32 devices in a mesh: dp: 8 (over y, x, core), head: 4 (over z).
Axes of the slice: x: 2, y: 2, z: 4, core: 2. Of those that a mesh axis runs over, the one named last changes fastest.
Arguments:
- tokens: bfloat16 [16384, 1024], P(('dp', 'head')), may hold values from -6 to 6
- input_norm_gain: float32 [1024], replicated, may hold values from 0.5 to 1.5
- proj_in: bfloat16 [1024, 8, 4, 128], P(None, 'head'), may hold values from -0.1875 to 0.1875
- proj_out: bfloat16 [8, 128, 1024], P('head'), may hold values from -0.1875 to 0.1875
- bias_slope: float32 [8], P('head'), may hold values from -0.8 to 0.3
- lengths: int32 [8, 16], P('dp'), may hold values from 1 to 1024, 2048 in all within a row
- cotangent: bfloat16 [16384, 1024], P(('dp', 'head')), may hold values from -6 to 6
Outputs:
- mixed: bfloat16 [16384, 1024], P(('dp', 'head'))
- token_gradient: float32 [16384, 1024], P(('dp', 'head'))
- norm_gain_gradient: float32 [1024], replicated
- grad_proj_in: float32 [1024, 8, 4, 128], P(None, 'head')
- grad_proj_out: float32 [8, 128, 1024], P('head')
- grad_slope: float32 [8], P('head')
The draws below stay inside these ranges and needn't reach their ends.
Inputs may be any that keep to these rules, and one draw needn't show every extreme that they name: Each row of lengths lists the history lengths of the 16 users of one group, summing to 2048; the longest in every row is exactly 1024.
All inputs are finite; a program needn't handle non-finite values.
Results may differ from the reference program's by a relative error of at most 0.034.
Values may be sent and summed in bfloat16 or wider, within the bound.
No kernel may reach another device: no remote copies, remote signals or barrier semaphores. Data moves between devices by JAX's collectives and lax.ppermute only.
A program may use at most 192 MiB of HBM per device.

```python
import math
import jax
import jax.numpy as jnp
import numpy as np
from jax import lax

D = 1024
HEADS = 8
HEAD_DIM = 128
GROUP_TOK = 2048
USERS = 16
MOST_LEN = 1024
TOKENS = 16384
N_DP = 8


def steps_of(own_key, dims, cuts, least, top_value):
    def one(axis_at, shards_of):
        heights = jax.random.uniform(jax.random.fold_in(jax.random.fold_in(own_key, 6), axis_at), (shards_of,), jnp.float32, least / len(cuts), top_value / len(cuts))
        return jnp.repeat(jnp.exp(heights), dims[axis_at] // shards_of).reshape((-1,) + (1,) * (len(dims) - axis_at - 1))

    loudness = one(*cuts[0])
    for cut in cuts[1:]:
        loudness = loudness * one(*cut)
    return loudness


def profile(number_of, total, reach, lean):
    portions = [(1 << 20) // math.isqrt(standing ** lean) + 1 for standing in range(2, number_of + 1)]
    spare, holding = total - reach - (number_of - 1), [1] * (number_of - 1)
    while spare > 0:
        movable = [i for i in range(number_of - 1) if holding[i] < reach]
        whole, budget = sum([portions[i] for i in movable]), spare
        for i in movable:
            addition = min(reach - holding[i], max(1, budget * portions[i] // whole), spare)
            holding[i] = holding[i] + addition
            spare = spare - addition
    return np.array([reach] + holding)


def uneven_parts(stream_key, count, total, limit, slope):
    if count == 2:
        one = jax.random.randint(stream_key, (), max(1, total - limit), min(limit, total - 1) + 1)
        return jnp.stack([one, total - one])
    sizes = jnp.asarray(profile(count, total, limit, slope), jnp.int32)
    couples = (count - 1) // 2
    donor, taker = sizes[1:1 + 2 * couples:2], sizes[2:2 + 2 * couples:2]
    margin = jnp.minimum(donor - 1, limit - taker)
    passed = jax.random.randint(jax.random.fold_in(stream_key, 1), (couples,), 0, 1 << 20) % (margin + 1)
    sizes = sizes.at[1:1 + 2 * couples:2].set(donor - passed).at[2:2 + 2 * couples:2].set(taker + passed)
    return sizes[jax.random.permutation(jax.random.fold_in(stream_key, 2), count)]


def bell_draw(key, shape, scale, limit, cuts=(), kind=jnp.bfloat16):
    gain = steps_of(key, shape, cuts, -0.22, 0.18) if cuts else 1.0
    entries = jax.random.normal(key, shape, jnp.float32) * scale * gain
    return jnp.minimum(jnp.maximum(entries, -limit), limit).astype(kind)


def setup_inputs(seed: int = 0) -> dict:
    streams_of = jax.random.split(jax.random.key(seed), 8)
    return {
        "tokens": bell_draw(streams_of[0], (TOKENS, D), 1.0, 6.0, ((0, 32),)),
        "input_norm_gain": jnp.clip(1.0 + 0.1 * jax.random.normal(streams_of[1], (D,), jnp.float32), 0.5, 1.5),
        "proj_in": bell_draw(streams_of[2], (D, HEADS, 4, HEAD_DIM), D ** -0.5, 0.1875, ((1, 4),)),
        "proj_out": bell_draw(streams_of[3], (HEADS, HEAD_DIM, D), D ** -0.5, 0.1875, ((0, 4),)),
        "bias_slope": jnp.clip(-0.8 + 1.1 * jax.random.uniform(streams_of[4], (HEADS,), jnp.float32) ** steps_of(streams_of[4], (HEADS,), ((0, 4),), -0.2, 0.2), -0.8, 0.3),
        "lengths": jax.vmap(lambda own: uneven_parts(own, USERS, GROUP_TOK, MOST_LEN, 2))(jax.random.split(streams_of[5], N_DP)).reshape((N_DP, USERS)).astype(jnp.int32),
        "cotangent": bell_draw(streams_of[6], (TOKENS, D), 1.0, 6.0, ((0, 32),)),
    }


EPSILON = 1e-05

def silu_slope(values):
    sigma = jax.nn.sigmoid(values)
    return sigma * (1.0 + values * (1.0 - sigma))

def user_index(group_lengths, total):
    ends = jnp.cumsum(group_lengths.astype(jnp.int32)).astype(jnp.int32)
    positions = jnp.arange(total).astype(jnp.int32)
    return lax.optimization_barrier(jnp.sum((positions[:, None] >= ends[None, :]).astype(jnp.int32), axis=1)).astype(jnp.int32)

def block_scores(queries, key_rows, slopes, user, first_row, last_row):
    scale = queries.shape[-1] ** (-0.5)
    query_pos = jnp.arange(first_row, last_row).astype(jnp.int32)
    key_pos = jnp.arange(0, last_row).astype(jnp.int32)
    offset = query_pos[:, None] - key_pos[None, :]
    visible = (offset >= 0) & (user[first_row:last_row, None] == user[None, :last_row])
    distance = jnp.log1p(jnp.maximum(offset, 0).astype(jnp.float32))
    scores = jnp.einsum('qhd,khd->hqk', queries[first_row:last_row].astype(jnp.float32), key_rows[:last_row].astype(jnp.float32)) * scale
    scores = scores + slopes[:, None, None] * distance[None]
    return (scores, visible, distance)

def attend(queries, key_rows, value_rows, slopes, user, block_rows):
    pieces = []
    for block_index in range(queries.shape[0] // block_rows):
        first_row = block_index * block_rows
        last_row = first_row + block_rows
        scores, visible, distance = block_scores(queries, key_rows, slopes, user, first_row, last_row)
        weights = jnp.where(visible[None], jax.nn.silu(scores), 0.0).astype(jnp.bfloat16)
        pieces.append(jnp.einsum('hqk,khd->qhd', weights.astype(jnp.float32), value_rows[:last_row].astype(jnp.float32)).astype(jnp.bfloat16))
    return jnp.concatenate(pieces, axis=0)

def attend_back(queries, key_rows, value_rows, slopes, user, block_rows, d_attended):
    scale = queries.shape[-1] ** (-0.5)
    grad_q = jnp.zeros(queries.shape, jnp.float32)
    grad_k = jnp.zeros(queries.shape, jnp.float32)
    grad_v = jnp.zeros(queries.shape, jnp.float32)
    grad_s = jnp.zeros(slopes.shape, jnp.float32)
    for block_index in range(queries.shape[0] // block_rows):
        first_row = block_index * block_rows
        last_row = first_row + block_rows
        scores, visible, distance = block_scores(queries, key_rows, slopes, user, first_row, last_row)
        weights = jnp.where(visible[None], jax.nn.silu(scores), 0.0).astype(jnp.bfloat16)
        d_here = d_attended[first_row:last_row].astype(jnp.float32)
        d_weights = jnp.einsum('qhd,khd->hqk', d_here, value_rows[:last_row].astype(jnp.float32))
        d_score = jnp.where(visible[None], d_weights * silu_slope(scores), 0.0)
        grad_s = grad_s + lax.optimization_barrier(jnp.sum(d_score * distance[None], axis=(1, 2)))
        d_narrow = d_score.astype(jnp.bfloat16).astype(jnp.float32)
        grad_v = grad_v.at[:last_row].add(jnp.einsum('hqk,qhd->khd', weights.astype(jnp.float32), d_here))
        grad_k = grad_k.at[:last_row].add(jnp.einsum('hqk,qhd->khd', d_narrow, queries[first_row:last_row].astype(jnp.float32)) * scale)
        grad_q = grad_q.at[first_row:last_row].add(jnp.einsum('hqk,khd->qhd', d_narrow, key_rows[:last_row].astype(jnp.float32)) * scale)
    return (grad_q, grad_k, grad_v, grad_s)

def group_pass(group_tokens, group_cot, group_lengths, input_norm_gain, proj_in, proj_out, bias_slope):
    total, width = group_tokens.shape
    token_single = group_tokens.astype(jnp.float32)
    centred_input = lax.optimization_barrier(jnp.mean(token_single, axis=1, keepdims=True))
    spread = lax.optimization_barrier(jnp.mean((token_single - centred_input) ** 2, axis=1, keepdims=True))
    inverse_deviation = lax.rsqrt(spread + EPSILON)
    standardized_input = (token_single - centred_input) * inverse_deviation
    norm_output = (standardized_input * input_norm_gain).astype(jnp.bfloat16)
    pre = jnp.einsum('gd,dhcj->ghcj', norm_output.astype(jnp.float32), proj_in.astype(jnp.float32))
    act = jax.nn.silu(pre).astype(jnp.bfloat16)
    gate_part = act[:, :, 0]
    value_rows = act[:, :, 1]
    queries = act[:, :, 2]
    key_rows = act[:, :, 3]
    user = user_index(group_lengths, total)
    block_rows = min(512, total)
    attended = attend(queries, key_rows, value_rows, bias_slope, user, block_rows)
    att_float = attended.astype(jnp.float32)
    mean_o = lax.optimization_barrier(jnp.sum(att_float, axis=(1, 2))) / width
    square_o = lax.optimization_barrier(jnp.sum(att_float * att_float, axis=(1, 2))) / width
    inv_o = lax.rsqrt(square_o - mean_o * mean_o + EPSILON)[:, None, None]
    normed_o = (att_float - mean_o[:, None, None]) * inv_o
    gated = (normed_o * gate_part.astype(jnp.float32)).astype(jnp.bfloat16)
    mixed = (token_single + jnp.einsum('ghj,hjd->gd', gated.astype(jnp.float32), proj_out.astype(jnp.float32))).astype(jnp.bfloat16)
    cotangent_single = group_cot.astype(jnp.float32)
    d_gated = jnp.einsum('gd,hjd->ghj', cotangent_single, proj_out.astype(jnp.float32))
    d_norm_in = d_gated * gate_part.astype(jnp.float32)
    d_gate = (d_gated * normed_o).astype(jnp.bfloat16)
    first_g = lax.optimization_barrier(jnp.sum(d_norm_in, axis=(1, 2))) / width
    second_g = lax.optimization_barrier(jnp.sum(d_norm_in * normed_o, axis=(1, 2))) / width
    d_attended = (inv_o * (d_norm_in - first_g[:, None, None] - normed_o * second_g[:, None, None])).astype(jnp.bfloat16)
    grad_q, grad_k, grad_v, grad_s = attend_back(queries, key_rows, value_rows, bias_slope, user, block_rows, d_attended)
    d_act = jnp.stack([d_gate.astype(jnp.float32), grad_v, grad_q, grad_k], axis=2)
    d_pre = (d_act * silu_slope(pre)).astype(jnp.bfloat16)
    grad_norm_output = jnp.einsum('ghcj,dhcj->gd', d_pre.astype(jnp.float32), proj_in.astype(jnp.float32))
    in_part = jnp.einsum('gd,ghcj->dhcj', norm_output.astype(jnp.float32), d_pre.astype(jnp.float32))
    out_part = jnp.einsum('ghj,gd->hjd', gated.astype(jnp.float32), cotangent_single)
    gain_grad_piece = lax.optimization_barrier(jnp.sum(grad_norm_output * standardized_input, axis=0))
    grad_standardized = grad_norm_output * input_norm_gain
    token_gradient = cotangent_single + inverse_deviation * (grad_standardized - lax.optimization_barrier(jnp.mean(grad_standardized, axis=1, keepdims=True)) - standardized_input * lax.optimization_barrier(jnp.mean(grad_standardized * standardized_input, axis=1, keepdims=True)))
    return (mixed, token_gradient, gain_grad_piece, in_part, out_part, grad_s)

def reference(tokens, input_norm_gain, proj_in, proj_out, bias_slope, lengths, cotangent):
    group_tokens = tokens.reshape(N_DP, GROUP_TOK, D)
    group_cots = cotangent.reshape(N_DP, GROUP_TOK, D)

    def one_group(carry, inputs):
        mixed, token_gradient, gain_grad_piece, in_part, out_part, slope_part = group_pass(inputs[0], inputs[1], inputs[2], input_norm_gain, proj_in, proj_out, bias_slope)
        carry = (carry[0] + gain_grad_piece, carry[1] + in_part, carry[2] + out_part, carry[3] + slope_part)
        return (carry, (mixed, token_gradient))
    start_carry = (jnp.zeros((D,), jnp.float32), jnp.zeros(proj_in.shape, jnp.float32), jnp.zeros(proj_out.shape, jnp.float32), jnp.zeros((HEADS,), jnp.float32))
    sums, outputs = lax.scan(one_group, start_carry, (group_tokens, group_cots, lengths))
    mixed = outputs[0].reshape(TOKENS, D)
    token_gradient = outputs[1].reshape(TOKENS, D)
    return (mixed, token_gradient, sums[0], sums[1], sums[2], sums[3])
```

```python
import functools

import jax
import jax.numpy as jnp
from jax import lax
from jax.experimental import pallas as pl
from jax.experimental.pallas import tpu as pltpu
from jax.sharding import PartitionSpec as P

EPSILON = 1e-05
BF = jnp.bfloat16
F32 = jnp.float32
AXES = ("dp", "head")
NT = (((1,), (1,)), ((), ()))
TN = (((0,), (0,)), ((), ()))
NN = (((1,), (0,)), ((), ()))


def dot(a, b, dims=NN):
    return lax.dot_general(a, b, dims, preferred_element_type=F32)


def silu_slope(values):
    sigma = jax.nn.sigmoid(values)
    return sigma * (1.0 + values * (1.0 - sigma))


def tanh_slope(values):
    sigma = 0.5 + 0.5 * jnp.tanh(0.5 * values)
    return sigma * (1.0 + values * (1.0 - sigma))


def fill_distance(dist, blocks, rows):
    row = lax.broadcasted_iota(jnp.int32, (rows, rows), 0)
    column = lax.broadcasted_iota(jnp.int32, (rows, rows), 1)

    def one(step, carry):
        offset = jnp.maximum(step * rows + row - column, 0).astype(F32)
        dist[step] = jnp.log(1.0 + offset)
        return carry

    lax.fori_loop(0, blocks, one, 0)


def half_score(q, k, slope, distance, visible, scale):
    u = dot(q, k, NT) * (0.5 * scale) + (0.5 * slope) * distance
    return jnp.where(visible, u, -1.0e4)


def visible_pairs(starts_ref, i, j, rows):
    row = lax.broadcasted_iota(jnp.int32, (rows, rows), 0) + i * rows
    column = lax.broadcasted_iota(jnp.int32, (rows, rows), 1) + j * rows
    first = starts_ref[pl.ds(pl.multiple_of(i * rows, rows), rows), :]
    return (column >= first) & (column <= row)


def forward_kernel(
    nh, dim, rows, blocks, low, held, sent, slopes, starts_ref, act_ref, out_ref, dist, acc
):
    fill_distance(dist, blocks, rows)
    scale = dim ** (-0.5)
    part = nh * dim

    def at(block):
        return pl.ds(pl.multiple_of(block * rows, rows), rows)

    def query_block(i, carry):
        acc[...] = jnp.zeros_like(acc)

        def key_block(j, inner):
            visible = visible_pairs(starts_ref, i, j, rows)
            distance = dist[i - j]
            for h in range(nh):
                q = act_ref[at(held[i]), part + h * dim : part + (h + 1) * dim]
                k = act_ref[at(held[j]), 2 * part + h * dim : 2 * part + (h + 1) * dim]
                v = act_ref[at(held[j]), h * dim : (h + 1) * dim]
                u = half_score(q, k, slopes[h], distance, visible, scale)
                w = (u + u * jnp.tanh(u)).astype(BF)
                acc[:, h * dim : (h + 1) * dim] += dot(w, v)
            return inner

        lax.fori_loop(low[i], i + 1, key_block, 0)
        out_ref[at(sent[i]), :] = acc[...].astype(BF)
        return carry

    lax.fori_loop(0, blocks, query_block, 0)


def backward_kernel(
    nh, dim, rows, blocks, low, held, sent, slopes, starts_ref, act_ref, pre_ref, datt_ref,
    out_ref, slope_ref, dist, dq, dk, dv, gs
):
    fill_distance(dist, blocks, rows)
    scale = dim ** (-0.5)
    part = nh * dim
    dk[...] = jnp.zeros_like(dk)
    dv[...] = jnp.zeros_like(dv)
    gs[...] = jnp.zeros_like(gs)

    def at(block):
        return pl.ds(pl.multiple_of(block * rows, rows), rows)

    def query_block(i, carry):
        dq[...] = jnp.zeros_like(dq)
        mine = held[i]

        def key_block(j, inner):
            visible = visible_pairs(starts_ref, i, j, rows)
            distance = dist[i - j]
            theirs = held[j]
            for h in range(nh):
                cols = slice(h * dim, (h + 1) * dim)
                q = act_ref[at(mine), part + h * dim : part + (h + 1) * dim]
                k = act_ref[at(theirs), 2 * part + h * dim : 2 * part + (h + 1) * dim]
                v = act_ref[at(theirs), cols]
                da = datt_ref[at(sent[i]), cols]
                u = half_score(q, k, slopes[h], distance, visible, scale)
                t = jnp.tanh(u)
                w = u + u * t
                ds = dot(da, v, NT) * ((1.0 + t) + w * (1.0 - t))
                gs[h] += jnp.sum((ds * distance).reshape(rows // 8, 8, rows), axis=0)
                wb = w.astype(BF)
                db = ds.astype(BF)
                dv[at(theirs), cols] += dot(wb, da, TN)
                dk[at(theirs), cols] += dot(db, q, TN)
                dq[:, cols] += dot(db, k)
            return inner

        lax.fori_loop(low[i], i + 1, key_block, 0)
        slope = tanh_slope(pre_ref[at(mine), part : 2 * part].astype(F32))
        out_ref[at(mine), part : 2 * part] = (dq[...] * (0.5 * scale) * slope).astype(BF)
        return carry

    lax.fori_loop(0, blocks, query_block, 0)

    def finish(b, carry):
        slope_v = tanh_slope(pre_ref[at(b), :part].astype(F32))
        out_ref[at(b), :part] = (dv[at(b), :] * slope_v).astype(BF)
        slope_k = tanh_slope(pre_ref[at(b), 2 * part :].astype(F32))
        out_ref[at(b), 2 * part :] = (dk[at(b), :] * (0.5 * scale) * slope_k).astype(BF)
        return carry

    lax.fori_loop(0, blocks, finish, 0)
    for h in range(nh):
        slope_ref[h] = 0.5 * gs[h]


def attention_cost(nh, dim, total, matmuls):
    pairs = total * total // 5
    return pl.CostEstimate(
        flops=2 * matmuls * nh * dim * pairs,
        bytes_accessed=total * nh * dim * 2 * 2 * matmuls,
        transcendentals=nh * pairs,
    )


def attend(nh, dim, rows, tables, slopes, starts, act):
    total = act.shape[0]
    blocks = total // rows
    smem = pl.BlockSpec(memory_space=pltpu.SMEM)
    vmem = pl.BlockSpec(memory_space=pltpu.VMEM)
    return pl.pallas_call(
        functools.partial(forward_kernel, nh, dim, rows, blocks),
        out_shape=jax.ShapeDtypeStruct((total, nh * dim), BF),
        in_specs=[smem] * 4 + [vmem] * 2,
        out_specs=vmem,
        scratch_shapes=[
            pltpu.VMEM((blocks, rows, rows), F32),
            pltpu.VMEM((rows, nh * dim), F32),
        ],
        compiler_params=pltpu.CompilerParams(vmem_limit_bytes=40 * 2**20),
        cost_estimate=attention_cost(nh, dim, total, 2),
    )(*tables, slopes, starts, act)


def attend_back(nh, dim, rows, tables, slopes, starts, act, pre, d_attended):
    total = act.shape[0]
    blocks = total // rows
    smem = pl.BlockSpec(memory_space=pltpu.SMEM)
    vmem = pl.BlockSpec(memory_space=pltpu.VMEM)
    return pl.pallas_call(
        functools.partial(backward_kernel, nh, dim, rows, blocks),
        out_shape=(
            jax.ShapeDtypeStruct(act.shape, BF),
            jax.ShapeDtypeStruct((nh, 8, rows), F32),
        ),
        in_specs=[smem] * 4 + [vmem] * 4,
        out_specs=(vmem, vmem),
        scratch_shapes=[
            pltpu.VMEM((blocks, rows, rows), F32),
            pltpu.VMEM((rows, nh * dim), F32),
            pltpu.VMEM((total, nh * dim), F32),
            pltpu.VMEM((total, nh * dim), F32),
            pltpu.VMEM((nh, 8, rows), F32),
        ],
        compiler_params=pltpu.CompilerParams(vmem_limit_bytes=48 * 2**20),
        cost_estimate=attention_cost(nh, dim, total, 5),
    )(*tables, slopes, starts, act, pre, d_attended)


def body(
    n_dp, n, tokens, input_norm_gain, proj_in, proj_out, bias_slope, lengths, cotangent
):
    local_rows, width = tokens.shape
    nh, dim = proj_in.shape[1], proj_in.shape[3]
    part = nh * dim
    rows = local_rows // 2
    half = n // 2
    dp = lax.axis_index("dp")
    z = lax.axis_index("head")
    c = dp & 1
    host = (z >= half).astype(jnp.int32)
    is_home = c == host

    def move(x, target):
        pairs = []
        for d in range(n_dp):
            for s in range(n):
                e, t = target(d, s)
                pairs.append((d * n + s, e * n + t))
        return lax.ppermute(x, AXES, pairs)

    def core_swap(x):
        return move(x, lambda d, s: (d ^ 1, s))

    def z_swap(x, bit):
        return move(x, lambda d, s: (d, s ^ bit))

    def dp_swap(x, bit):
        return move(x, lambda d, s: (d ^ bit, s))

    def send_target(r):
        def target(d, s):
            core = int(s >= half)
            return ((d & ~1) | core, s ^ r ^ ((d & 1) * half))

        return target

    def back_target(r):
        forward = {}
        for d in range(n_dp):
            for s in range(n):
                forward[send_target(r)(d, s)] = (d, s)
        return lambda d, s: forward[(d, s)]

    def cross(x):
        return move(x, lambda d, s: (d, s ^ ((d & 1) * half)))

    token_single = tokens.astype(F32)
    centred_input = jnp.mean(token_single, axis=1, keepdims=True)
    spread = jnp.mean((token_single - centred_input) ** 2, axis=1, keepdims=True)
    inverse_deviation = lax.rsqrt(spread + EPSILON)
    xhat = (token_single - centred_input) * inverse_deviation
    normed = (xhat * input_norm_gain).astype(BF)

    first, second = normed[:rows], normed[rows:]
    keep = jnp.where(c == 0, first, second)
    give = jnp.where(c == 0, second, first)
    got = core_swap(give)
    items = {0: jnp.where(is_home, keep, got)}
    items[half] = z_swap(jnp.where(is_home, got, keep), half)
    bit = 1
    while bit < half:
        for t in [t for t in sorted(items) if not t & bit]:
            items[t ^ bit] = z_swap(items[t], bit)
        bit *= 2
    mine = [items[t] for t in range(n)]
    theirs = [core_swap(x) for x in mine]
    gathered = jnp.concatenate(mine + theirs, axis=0)
    total = gathered.shape[0]

    w_all = proj_in.transpose(0, 2, 1, 3).reshape(width, 4 * part)
    w_own = w_all[:, part:]
    slab = width // n_dp
    piece = z_swap(lax.dynamic_slice_in_dim(w_own, dp * slab, slab, 0), half)
    bits = [1 << b for b in range(n_dp.bit_length() - 1)]

    def dp_double(x, bit):
        other = dp_swap(x, bit)
        up = (dp & bit) != 0
        return jnp.concatenate([jnp.where(up, other, x), jnp.where(up, x, other)], axis=0)

    for b in bits:
        piece = dp_double(piece, b)
    w_qkv = jnp.where(c == 0, w_own, piece)

    def over_heads(x):
        parts = {0: x}
        step = 1
        while step < n:
            for t in sorted(parts):
                parts[t ^ step] = z_swap(parts[t], step)
            step *= 2
        return jnp.stack([parts[t] for t in range(n)])

    slab_o = part // n_dp
    out_slab = lax.dynamic_slice_in_dim(proj_out.reshape(part, width), dp * slab_o, slab_o, 0)
    gate_slab = lax.dynamic_slice_in_dim(w_all[:, :part], dp * slab, slab, 0)
    w_out = lax.all_gather(over_heads(out_slab), "dp")
    w_out = w_out.transpose(1, 0, 2, 3).reshape(n * part, width)
    w_gate = lax.all_gather(over_heads(gate_slab), "dp")
    w_gate = w_gate.transpose(0, 2, 1, 3).reshape(width, n * part)

    own_lengths = lengths[0]
    hosted_lengths = jnp.where(is_home, own_lengths, core_swap(own_lengths))
    ends = jnp.cumsum(hosted_lengths)
    positions = jnp.arange(total, dtype=jnp.int32)
    starts = jnp.max(
        jnp.where(positions[:, None] >= ends[None, :], ends[None, :], 0), axis=1, keepdims=True
    ).astype(jnp.int32)
    block = jnp.arange(total // rows, dtype=jnp.int32)
    low = starts[::rows, 0] // rows
    shard = (block // 2) ^ z
    held = ((block & 1) ^ c) * n + shard
    sent = 2 * (shard ^ (c * half)) + (block & 1)
    tables = (low, held, sent)
    slopes = cross(bias_slope)

    pre = dot(gathered, w_qkv)
    act = jax.nn.silu(pre).astype(BF)
    pre = pre.astype(BF)
    attended = attend(nh, dim, rows, tables, slopes, starts, act)
    att_own = jnp.concatenate(
        [
            move(attended[r * local_rows : (r + 1) * local_rows], send_target(r))
            for r in range(n)
        ],
        axis=1,
    ).astype(F32)

    pre_gate = dot(normed, w_gate)
    gate = jax.nn.silu(pre_gate).astype(BF).astype(F32)
    d_gated = dot(cotangent, w_out, NT)
    mean_o = jnp.mean(att_own, axis=1, keepdims=True)
    square_o = jnp.mean(att_own * att_own, axis=1, keepdims=True)
    inv_o = lax.rsqrt(square_o - mean_o * mean_o + EPSILON)
    normed_o = (att_own - mean_o) * inv_o
    gated = (normed_o * gate).astype(BF)
    d_norm_in = d_gated * gate
    first_g = jnp.mean(d_norm_in, axis=1, keepdims=True)
    second_g = jnp.mean(d_norm_in * normed_o, axis=1, keepdims=True)
    d_attended = (inv_o * (d_norm_in - first_g - normed_o * second_g)).astype(BF)
    d_att = jnp.concatenate(
        [move(d_attended[:, r * part : (r + 1) * part], back_target(r)) for r in range(n)],
        axis=0,
    )
    mixed = (token_single + dot(gated, w_out)).astype(BF)
    d_gate = (d_gated * normed_o).astype(BF).astype(F32)
    d_pre_gate = (d_gate * silu_slope(pre_gate)).astype(BF)
    d_normed_gate = dot(d_pre_gate, w_gate, NT)
    gate_part = dot(normed, d_pre_gate, TN)
    out_part = dot(gated, cotangent, TN)

    def reduce_heads(parts):
        step = n // 2
        while step >= 1:
            for t in range(step):
                other = z_swap(parts[t ^ step], step)
                parts[t] = (parts[t].astype(F32) + other.astype(F32)).astype(BF)
            step //= 2
        return parts[0]

    gate_sum = lax.psum_scatter(
        gate_part.astype(BF), "dp", scatter_dimension=0, tiled=True
    )
    gate_sum = reduce_heads([gate_sum[:, t * part : (t + 1) * part] for t in range(n)])
    grad_gate = lax.all_gather(gate_sum, "dp", axis=0, tiled=True)
    out_sum = lax.psum_scatter(
        out_part.astype(BF).reshape(n, part, width), "dp", scatter_dimension=1, tiled=True
    )
    out_sum = reduce_heads([out_sum[t] for t in range(n)])
    grad_out = lax.all_gather(out_sum, "dp", axis=0, tiled=True)

    d_pre, slope_rows = attend_back(
        nh, dim, rows, tables, slopes, starts, act, pre, d_att
    )
    in_part = dot(gathered, d_pre, TN)

    partial = dot(d_pre, w_qkv, NT).astype(BF)
    blocks = [partial[b * rows : (b + 1) * rows] for b in range(2 * n)]

    def add(x, y):
        return (x.astype(F32) + y.astype(F32)).astype(BF)

    sums = [add(blocks[t], core_swap(blocks[n + t])) for t in range(n)]
    bit = half // 2
    while bit >= 1:
        for t in [u for u in range(n) if (u & (half - 1)) < bit]:
            sums[t] = add(sums[t], z_swap(sums[t ^ bit], bit))
        bit //= 2
    home, away = sums[0], z_swap(sums[half], half)
    keep = jnp.where(is_home, home, away)
    got = core_swap(jnp.where(is_home, away, home))
    d_normed = jnp.concatenate(
        [jnp.where(c == 0, keep, got), jnp.where(c == 0, got, keep)], axis=0
    ).astype(F32) + d_normed_gate

    x = in_part.astype(BF)
    for b in bits[1:]:
        size = x.shape[0] // 2
        up = (dp & b) != 0
        x = add(
            jnp.where(up, x[size:], x[:size]),
            dp_swap(jnp.where(up, x[:size], x[size:]), b),
        )
    x = cross(x)
    size = x.shape[0] // 2
    x = add(
        jnp.where(c == 0, x[:size], x[size:]),
        core_swap(jnp.where(c == 0, x[size:], x[:size])),
    )
    x = x[None]
    for b in bits[:0:-1]:
        x = dp_double(x, b)
    other = core_swap(x)
    x = jnp.stack([jnp.where(c == 0, x, other), jnp.where(c == 0, other, x)], axis=1)
    grad_qkv = x.reshape(width, 3, nh, dim)
    grad_proj_in = jnp.concatenate(
        [grad_gate.reshape(width, nh, 1, dim), grad_qkv.transpose(0, 2, 1, 3)], axis=2
    ).astype(F32)
    grad_proj_out = grad_out.reshape(nh, dim, width).astype(F32)

    gain_part = jnp.sum(in_part * w_qkv.astype(F32), axis=1)
    gain_part = (gain_part + jnp.sum(gate_part * w_gate.astype(F32), axis=1)) / input_norm_gain
    own_slope = jnp.sum(slope_rows, axis=(1, 2))
    chunk = z ^ (c * half)
    slope_part = jnp.where(jnp.arange(n)[:, None] == chunk, own_slope[None, :], 0.0)
    small = lax.psum(jnp.concatenate([gain_part, slope_part.reshape(-1)]), AXES)
    norm_gain_gradient = small[:width]
    grad_slope = lax.dynamic_slice_in_dim(small, width + z * nh, nh, 0)

    dh = d_normed * input_norm_gain
    token_gradient = cotangent.astype(F32) + inverse_deviation * (
        dh
        - jnp.mean(dh, axis=1, keepdims=True)
        - xhat * jnp.mean(dh * xhat, axis=1, keepdims=True)
    )
    return (mixed, token_gradient, norm_gain_gradient, grad_proj_in, grad_proj_out, grad_slope)


def solution(mesh):
    return jax.shard_map(
        functools.partial(body, mesh.shape["dp"], mesh.shape["head"]),
        mesh=mesh,
        in_specs=(
            P(("dp", "head"), None),
            P(),
            P(None, "head", None, None),
            P("head", None, None),
            P("head"),
            P("dp", None),
            P(("dp", "head"), None),
        ),
        out_specs=(
            P(("dp", "head"), None),
            P(("dp", "head"), None),
            P(),
            P(None, "head", None, None),
            P("head", None, None),
            P("head"),
        ),
        check_vma=False,
    )
```

```python
import functools

import jax
import jax.numpy as jnp
from jax import lax
from jax.experimental import pallas as pl
from jax.experimental.pallas import tpu as pltpu
from jax.sharding import PartitionSpec as P

EPSILON = 1e-05
BF = jnp.bfloat16
F32 = jnp.float32
AXES = ("dp", "head")
NT = (((1,), (1,)), ((), ()))
TN = (((0,), (0,)), ((), ()))
NN = (((1,), (0,)), ((), ()))


def dot(a, b, dims=NN):
    return lax.dot_general(a, b, dims, preferred_element_type=F32)


def silu_slope(values):
    sigma = jax.nn.sigmoid(values)
    return sigma * (1.0 + values * (1.0 - sigma))


def tanh_slope(values):
    sigma = 0.5 + 0.5 * jnp.tanh(0.5 * values)
    return sigma * (1.0 + values * (1.0 - sigma))


def fill_distance(dist, blocks, rows):
    row = lax.broadcasted_iota(jnp.int32, (rows, rows), 0)
    column = lax.broadcasted_iota(jnp.int32, (rows, rows), 1)

    def one(step, carry):
        offset = jnp.maximum(step * rows + row - column, 0).astype(F32)
        dist[step] = jnp.log(1.0 + offset)
        return carry

    lax.fori_loop(0, blocks, one, 0)


def half_score(q, k, slope, distance, visible, scale):
    u = dot(q, k, NT) * (0.5 * scale) + (0.5 * slope) * distance
    return jnp.where(visible, u, -1.0e4)


def visible_pairs(starts_ref, i, j, rows):
    row = lax.broadcasted_iota(jnp.int32, (rows, rows), 0) + i * rows
    column = lax.broadcasted_iota(jnp.int32, (rows, rows), 1) + j * rows
    first = starts_ref[pl.ds(pl.multiple_of(i * rows, rows), rows), :]
    return (column >= first) & (column <= row)


def forward_kernel(
    nh, dim, rows, blocks, low, held, sent, slopes, starts_ref, w_ref, *refs
):
    pieces = refs[:blocks]
    out_ref, act_ref, pre_ref, dist, acc = refs[blocks:]
    for b in range(blocks):
        pre = dot(pieces[b][...], w_ref[...], NT)
        half = 0.5 * pre
        pre_ref[b * rows : (b + 1) * rows, :] = pre.astype(BF)
        act_ref[b * rows : (b + 1) * rows, :] = (half + half * jnp.tanh(half)).astype(BF)
    fill_distance(dist, blocks, rows)
    scale = dim ** (-0.5)
    part = nh * dim

    def at(block):
        return pl.ds(pl.multiple_of(block * rows, rows), rows)

    def query_block(i, carry):
        acc[...] = jnp.zeros_like(acc)

        def key_block(j, inner):
            visible = visible_pairs(starts_ref, i, j, rows)
            distance = dist[i - j]
            for h in range(nh):
                q = act_ref[at(held[i]), part + h * dim : part + (h + 1) * dim]
                k = act_ref[at(held[j]), 2 * part + h * dim : 2 * part + (h + 1) * dim]
                v = act_ref[at(held[j]), h * dim : (h + 1) * dim]
                u = half_score(q, k, slopes[h], distance, visible, scale)
                w = (u + u * jnp.tanh(u)).astype(BF)
                acc[:, h * dim : (h + 1) * dim] += dot(w, v)
            return inner

        lax.fori_loop(low[i], i + 1, key_block, 0)
        out_ref[at(sent[i]), :] = acc[...].astype(BF)
        return carry

    lax.fori_loop(0, blocks, query_block, 0)


def backward_kernel(
    nh, dim, rows, blocks, low, held, sent, slopes, starts_ref, act_ref, pre_ref, datt_ref,
    out_ref, slope_ref, dist, dq, dk, dv, gs
):
    fill_distance(dist, blocks, rows)
    scale = dim ** (-0.5)
    part = nh * dim
    dk[...] = jnp.zeros_like(dk)
    dv[...] = jnp.zeros_like(dv)
    gs[...] = jnp.zeros_like(gs)

    def at(block):
        return pl.ds(pl.multiple_of(block * rows, rows), rows)

    def query_block(i, carry):
        dq[...] = jnp.zeros_like(dq)
        mine = held[i]

        def key_block(j, inner):
            visible = visible_pairs(starts_ref, i, j, rows)
            distance = dist[i - j]
            theirs = held[j]
            for h in range(nh):
                cols = slice(h * dim, (h + 1) * dim)
                q = act_ref[at(mine), part + h * dim : part + (h + 1) * dim]
                k = act_ref[at(theirs), 2 * part + h * dim : 2 * part + (h + 1) * dim]
                v = act_ref[at(theirs), cols]
                da = datt_ref[at(sent[i]), cols]
                u = half_score(q, k, slopes[h], distance, visible, scale)
                t = jnp.tanh(u)
                w = u + u * t
                ds = dot(da, v, NT) * ((1.0 + t) + w * (1.0 - t))
                gs[h] += jnp.sum((ds * distance).reshape(rows // 8, 8, rows), axis=0)
                wb = w.astype(BF)
                db = ds.astype(BF)
                dv[at(theirs), cols] += dot(wb, da, TN)
                dk[at(theirs), cols] += dot(db, q, TN)
                dq[:, cols] += dot(db, k)
            return inner

        lax.fori_loop(low[i], i + 1, key_block, 0)
        slope = tanh_slope(pre_ref[at(mine), part : 2 * part].astype(F32))
        out_ref[at(mine), part : 2 * part] = (dq[...] * (0.5 * scale) * slope).astype(BF)
        return carry

    lax.fori_loop(0, blocks, query_block, 0)

    def finish(b, carry):
        slope_v = tanh_slope(pre_ref[at(b), :part].astype(F32))
        out_ref[at(b), :part] = (dv[at(b), :] * slope_v).astype(BF)
        slope_k = tanh_slope(pre_ref[at(b), 2 * part :].astype(F32))
        out_ref[at(b), 2 * part :] = (dk[at(b), :] * (0.5 * scale) * slope_k).astype(BF)
        return carry

    lax.fori_loop(0, blocks, finish, 0)
    for h in range(nh):
        slope_ref[h] = 0.5 * gs[h]


def attention_cost(nh, dim, total, matmuls):
    pairs = total * total // 5
    return pl.CostEstimate(
        flops=30 * matmuls * nh * dim * pairs,
        bytes_accessed=total * nh * dim * 2 * 2 * matmuls,
        transcendentals=nh * pairs,
    )


def attend(nh, dim, rows, tables, slopes, starts, w, pieces):
    blocks = len(pieces)
    total = blocks * rows
    wide = jax.ShapeDtypeStruct((total, 3 * nh * dim), BF)
    smem = pl.BlockSpec(memory_space=pltpu.SMEM)
    vmem = pl.BlockSpec(memory_space=pltpu.VMEM)
    return pl.pallas_call(
        functools.partial(forward_kernel, nh, dim, rows, blocks),
        out_shape=(jax.ShapeDtypeStruct((total, nh * dim), BF), wide, wide),
        in_specs=[smem] * 4 + [vmem] * (2 + blocks),
        out_specs=(vmem,) * 3,
        scratch_shapes=[
            pltpu.VMEM((blocks, rows, rows), F32),
            pltpu.VMEM((rows, nh * dim), F32),
        ],
        compiler_params=pltpu.CompilerParams(vmem_limit_bytes=40 * 2**20),
        cost_estimate=attention_cost(nh, dim, total, 2),
    )(*tables, slopes, starts, w, *pieces)


def unpack_kernel(nh, dim, w_ref, after_ref, own_ref, gate_ref):
    part = nh * dim
    for h in range(nh):
        for kind in range(4):
            x = w_ref[:, h * 4 + kind, :]
            x = x.astype(F32).T.astype(BF)
            at = ((kind - 1) * nh + h) * dim
            if kind:
                own_ref[at : at + dim, :] = x
            else:
                gate_ref[h * dim : (h + 1) * dim, :] = x


def unpack(nh, dim, proj_in, after):
    width = proj_in.shape[0]
    vmem = pl.BlockSpec(memory_space=pltpu.VMEM)
    return pl.pallas_call(
        functools.partial(unpack_kernel, nh, dim),
        out_shape=(
            jax.ShapeDtypeStruct((3 * nh * dim, width), BF),
            jax.ShapeDtypeStruct((nh * dim, width), BF),
        ),
        in_specs=[vmem, pl.BlockSpec(memory_space=pl.ANY)],
        out_specs=(vmem,) * 2,
        compiler_params=pltpu.CompilerParams(vmem_limit_bytes=24 * 2**20),
        cost_estimate=pl.CostEstimate(flops=2 * 10**10, bytes_accessed=8 * 2**20, transcendentals=0),
    )(proj_in.reshape(width, nh * 4, dim), after)


def prepare_kernel(
    n, n_dp, slab, z_ref, all_ref, normed_ref, cot_ref, after_ref,
    gate_w_ref, out_w_ref, pre_gate_ref, d_gated_ref
):
    part = n_dp * slab
    for t in range(n):
        q = z_ref[0] ^ t
        for s in range(n_dp):
            at = t * part + s * slab
            gate_w_ref[at : at + slab, :] = all_ref[s, q, 0]
            out_w_ref[at : at + slab, :] = all_ref[s, q, 1]
    for t in range(n):
        at = slice(t * part, (t + 1) * part)
        pre_gate_ref[:, at] = dot(normed_ref[...], gate_w_ref[at, :], NT)
        d_gated_ref[:, at] = dot(cot_ref[...], out_w_ref[at, :], NT)


def prepare(n, n_dp, slab, z, everything, normed, cotangent, after):
    rows, width = normed.shape
    vmem = pl.BlockSpec(memory_space=pltpu.VMEM)
    columns = n * n_dp * slab
    return pl.pallas_call(
        functools.partial(prepare_kernel, n, n_dp, slab),
        out_shape=(
            jax.ShapeDtypeStruct((columns, width), BF),
            jax.ShapeDtypeStruct((columns, width), BF),
            jax.ShapeDtypeStruct((rows, columns), F32),
            jax.ShapeDtypeStruct((rows, columns), F32),
        ),
        in_specs=[pl.BlockSpec(memory_space=pltpu.SMEM)]
        + [vmem] * 3
        + [pl.BlockSpec(memory_space=pl.ANY)],
        out_specs=(vmem,) * 4,
        compiler_params=pltpu.CompilerParams(vmem_limit_bytes=32 * 2**20),
        cost_estimate=pl.CostEstimate(
            flops=20 * rows * width * columns, bytes_accessed=16 * 2**20, transcendentals=0
        ),
    )(z.reshape(1), everything, normed, cotangent, after)


def assemble_kernel(nh, dim, n_dp, first_ref, second_ref, in_ref, out_ref, rows_ref):
    part = nh * dim
    slab = part // n_dp
    side = first_ref.shape[2]
    for s in range(n_dp):
        for side_at, ref in ((0, first_ref), (1, second_ref)):
            x = ref[s].astype(F32)
            columns = slice(side_at * side, (side_at + 1) * side)
            rows_ref[3 * s * slab : 3 * (s + 1) * slab, columns] = x[: 3 * slab]
            at = 3 * part + s * slab
            rows_ref[at : at + slab, columns] = x[3 * slab : 4 * slab]
            out_ref[s * slab : (s + 1) * slab, columns] = x[4 * slab : 5 * slab]
    for h in range(nh):
        for kind in range(4):
            at = kind * part + h * dim
            in_ref[:, h * 4 + (kind + 1) % 4, :] = rows_ref[at : at + dim, :].T


def assemble(nh, dim, n_dp, width, first, second):
    vmem = pl.BlockSpec(memory_space=pltpu.VMEM)
    return pl.pallas_call(
        functools.partial(assemble_kernel, nh, dim, n_dp),
        out_shape=(
            jax.ShapeDtypeStruct((width, nh * 4, dim), F32),
            jax.ShapeDtypeStruct((nh * dim, width), F32),
        ),
        in_specs=[vmem] * 2,
        out_specs=(vmem,) * 2,
        scratch_shapes=[pltpu.VMEM((4 * nh * dim, width), F32)],
        compiler_params=pltpu.CompilerParams(vmem_limit_bytes=40 * 2**20),
        cost_estimate=pl.CostEstimate(flops=0, bytes_accessed=8 * 2**20, transcendentals=0),
    )(first, second)


def attend_back(nh, dim, rows, tables, slopes, starts, act, pre, d_attended):
    total = act.shape[0]
    blocks = total // rows
    smem = pl.BlockSpec(memory_space=pltpu.SMEM)
    vmem = pl.BlockSpec(memory_space=pltpu.VMEM)
    return pl.pallas_call(
        functools.partial(backward_kernel, nh, dim, rows, blocks),
        out_shape=(
            jax.ShapeDtypeStruct(act.shape, BF),
            jax.ShapeDtypeStruct((nh, 8, rows), F32),
        ),
        in_specs=[smem] * 4 + [vmem] * 4,
        out_specs=(vmem, vmem),
        scratch_shapes=[
            pltpu.VMEM((blocks, rows, rows), F32),
            pltpu.VMEM((rows, nh * dim), F32),
            pltpu.VMEM((total, nh * dim), F32),
            pltpu.VMEM((total, nh * dim), F32),
            pltpu.VMEM((nh, 8, rows), F32),
        ],
        compiler_params=pltpu.CompilerParams(vmem_limit_bytes=48 * 2**20),
        cost_estimate=attention_cost(nh, dim, total, 5),
    )(*tables, slopes, starts, act, pre, d_attended)


def body(
    n_dp, n, tokens, input_norm_gain, proj_in, proj_out, bias_slope, lengths, cotangent
):
    local_rows, width = tokens.shape
    nh, dim = proj_in.shape[1], proj_in.shape[3]
    part = nh * dim
    rows = local_rows // 2
    half = n // 2
    dp = lax.axis_index("dp")
    z = lax.axis_index("head")
    c = dp & 1
    host = (z >= half).astype(jnp.int32)
    is_home = c == host

    def move(x, target):
        pairs = []
        for d in range(n_dp):
            for s in range(n):
                e, t = target(d, s)
                pairs.append((d * n + s, e * n + t))
        return lax.ppermute(x, AXES, pairs)

    def core_swap(x):
        return move(x, lambda d, s: (d ^ 1, s))

    def z_swap(x, bit):
        return move(x, lambda d, s: (d, s ^ bit))

    def dp_swap(x, bit):
        return move(x, lambda d, s: (d ^ bit, s))

    def send_target(r):
        def target(d, s):
            core = int(s >= half)
            return ((d & ~1) | core, s ^ r ^ ((d & 1) * half))

        return target

    def back_target(r):
        forward = {}
        for d in range(n_dp):
            for s in range(n):
                forward[send_target(r)(d, s)] = (d, s)
        return lambda d, s: forward[(d, s)]

    def cross(x):
        return move(x, lambda d, s: (d, s ^ ((d & 1) * half)))

    token_single = tokens.astype(F32)
    centred_input = jnp.mean(token_single, axis=1, keepdims=True)
    spread = jnp.mean((token_single - centred_input) ** 2, axis=1, keepdims=True)
    inverse_deviation = lax.rsqrt(spread + EPSILON)
    xhat = (token_single - centred_input) * inverse_deviation
    normed = (xhat * input_norm_gain).astype(BF)

    first, second = normed[:rows], normed[rows:]
    keep = jnp.where(c == 0, first, second)
    give = jnp.where(c == 0, second, first)
    barrier = lax.optimization_barrier
    bits = [1 << b for b in range(n_dp.bit_length() - 1)]
    slab_o = part // n_dp
    slab_w = 3 * slab_o
    got = core_swap(give)
    w_own, gate_rows = unpack(nh, dim, proj_in, give)
    mirrored = sum(
        jnp.where((dp & b) != 0, bits[-1] // b, 0) for b in bits
    )
    w_slab = lax.dynamic_slice_in_dim(w_own, mirrored * slab_w, slab_w, 0)
    items = {0: jnp.where(is_home, keep, got)}
    crossed = z_swap(
        jnp.concatenate([jnp.where(is_home, got, keep), w_slab], axis=0), half
    )
    bit = 1
    while bit < half:
        for t in sorted(items):
            items[t ^ bit] = z_swap(items[t], bit)
        bit *= 2
    items, crossed = barrier((items, crossed))
    items[half], piece = crossed[:rows], crossed[rows:]
    bit = 1
    while bit < half:
        for t in [t for t in sorted(items) if t >= half]:
            items[t ^ bit] = z_swap(items[t], bit)
        bit *= 2

    def dp_double(x, bit):
        other = dp_swap(x, bit)
        up = (dp & bit) != 0
        return jnp.concatenate([jnp.where(up, other, x), jnp.where(up, x, other)], axis=0)

    for b in bits[:1:-1]:
        piece = dp_double(piece, b)
    items, piece = barrier((items, piece))
    for b in bits[1::-1]:
        piece = dp_double(piece, b)
    mine = [items[t] for t in range(n)]
    theirs = [core_swap(x) for x in mine]
    total = n * local_rows

    slabs = jnp.concatenate(
        [
            lax.dynamic_slice_in_dim(gate_rows, dp * slab_o, slab_o, 0),
            lax.dynamic_slice_in_dim(proj_out.reshape(part, width), dp * slab_o, slab_o, 0),
        ],
        axis=0,
    )
    everything = lax.all_gather(slabs, AXES).reshape(n_dp, n, 2, slab_o, width)

    w_qkv = jnp.where(c == 0, w_own, piece)

    own_lengths = lengths[0]
    hosted_lengths = jnp.where(is_home, own_lengths, core_swap(own_lengths))
    ends = jnp.cumsum(hosted_lengths)
    positions = jnp.arange(total, dtype=jnp.int32)
    starts = jnp.max(
        jnp.where(positions[:, None] >= ends[None, :], ends[None, :], 0), axis=1, keepdims=True
    ).astype(jnp.int32)
    block = jnp.arange(total // rows, dtype=jnp.int32)
    low = starts[::rows, 0] // rows
    shard = (block // 2) ^ z
    held = ((block & 1) ^ c) * n + shard
    sent = 2 * (shard ^ (c * half)) + (block & 1)
    tables = (low, held, sent)
    slopes = cross(bias_slope)

    attended, act, pre = attend(
        nh, dim, rows, tables, slopes, starts, w_qkv, mine + theirs
    )
    w_gate, w_out, pre_gate, d_gated = prepare(
        n, n_dp, slab_o, z, everything, normed, cotangent, attended
    )
    gathered = jnp.concatenate(mine + theirs, axis=0)
    arrived = [
        move(attended[r * local_rows : (r + 1) * local_rows], send_target(r)) for r in range(n)
    ]
    arrived, w_gate, w_out, pre_gate, d_gated = barrier(
        (arrived, w_gate, w_out, pre_gate, d_gated)
    )
    att_own = jnp.concatenate(arrived, axis=1).astype(F32)

    gate = jax.nn.silu(pre_gate).astype(BF).astype(F32)
    mean_o = jnp.mean(att_own, axis=1, keepdims=True)
    square_o = jnp.mean(att_own * att_own, axis=1, keepdims=True)
    inv_o = lax.rsqrt(square_o - mean_o * mean_o + EPSILON)
    normed_o = (att_own - mean_o) * inv_o
    gated = (normed_o * gate).astype(BF)
    d_norm_in = d_gated * gate
    first_g = jnp.mean(d_norm_in, axis=1, keepdims=True)
    second_g = jnp.mean(d_norm_in * normed_o, axis=1, keepdims=True)
    d_attended = (inv_o * (d_norm_in - first_g - normed_o * second_g)).astype(BF)
    mixed = (token_single + dot(gated, w_out)).astype(BF)
    d_gate = (d_gated * normed_o).astype(BF).astype(F32)
    d_pre_gate = (d_gate * silu_slope(pre_gate)).astype(BF)
    d_normed_gate = dot(d_pre_gate, w_gate)
    gate_part = dot(d_pre_gate, normed, TN)
    out_part = dot(gated, cotangent, TN)

    def add(x, y):
        return (x.astype(F32) + y.astype(F32)).astype(BF)

    order = bits[1:] + bits[:1]
    split = [2] * len(bits)
    forth, back = bits[1:], bits[:0:-1]

    def reduce_bit(x, b, axis):
        up = (dp & b) != 0
        low_half = lax.slice_in_dim(x, 0, 1, axis=axis)
        high_half = lax.slice_in_dim(x, 1, 2, axis=axis)
        return add(
            jnp.where(up, high_half, low_half),
            dp_swap(jnp.where(up, low_half, high_half), b),
        )

    def double_bit(x, b, axis):
        other = dp_swap(x, b)
        up = (dp & b) != 0
        return jnp.concatenate(
            [jnp.where(up, other, x), jnp.where(up, x, other)], axis=axis
        )

    both = jnp.stack([gate_part, out_part]).astype(BF)
    both = both.reshape([2, n] + split + [slab_o, width])
    d_attended, both = barrier((d_attended, both))
    both = reduce_bit(both, 1, 1 + len(bits))
    arrived = [
        move(d_attended[:, r * part : (r + 1) * part], back_target(r)) for r in range(n)
    ]
    d_att = jnp.concatenate(arrived, axis=0)
    pair = [both[0], both[1]]
    d_att, pair = lax.optimization_barrier((d_att, pair))
    def reduce_pair(pair, k, first_axis):
        return [
            reduce_bit(pair[0], forth[k], first_axis + order.index(forth[k])),
            reduce_bit(pair[1], back[k], first_axis + order.index(back[k])),
        ]

    both = reduce_pair(pair, 0, 1)

    d_pre, slope_rows = attend_back(
        nh, dim, rows, tables, slopes, starts, act, pre, d_att
    )

    def partial(first_block, last_block):
        return dot(d_pre[first_block * rows : last_block * rows], w_qkv).astype(BF)

    d_pre, both = barrier((d_pre, both))
    theirs = partial(n, 2 * n)
    got = core_swap(theirs)
    d_pre, theirs = barrier((d_pre, theirs))
    in_part = dot(d_pre, gathered, TN).astype(BF)
    mine = partial(0, n)
    for k in range(1, len(forth)):
        both = reduce_pair(both, k, 1)
    both = jnp.stack(both).reshape(2, n, slab_o, width)
    in_part, got, both = barrier((in_part, got, both))

    side = width // 2
    x = in_part.reshape(split + [slab_w, width])
    pair = reduce_pair([x[..., :side], x[..., side:]], 0, 0)
    home, away = add(mine[: half * rows], got[: half * rows]), add(
        mine[half * rows :], got[half * rows :]
    )
    bit = half // 2
    while bit >= 1:
        away = add(away[: bit * rows], z_swap(away[bit * rows :], bit))
        bit //= 2
    both = add(both[:, :half], z_swap(both[:, half:], half))
    for k in range(1, len(forth)):
        pair = reduce_pair(pair, k, 0)
    pair, away, home, both = barrier((pair, away, home, both))

    cuts = [away[k * rows // 4 : (k + 1) * rows // 4] for k in range(4)]
    moved = [z_swap(cuts[0], half)]
    bit = half // 2
    while bit >= 1:
        home = add(home[: bit * rows], z_swap(home[bit * rows :], bit))
        both = add(both[:, :bit], z_swap(both[:, bit:], bit))
        bit //= 2
    both = both.reshape(2 * slab_o, width)
    x = cross(jnp.concatenate(pair, axis=-1))
    x, moved, home, both, cuts = barrier((x, moved, home, both, cuts))

    moved.append(z_swap(cuts[1], half))
    x = reduce_bit(x, 1, len(bits) - 1)
    x, moved, cuts = barrier((x, moved, cuts))
    moved.append(z_swap(cuts[2], half))
    x = x.reshape(slab_w, width)
    place = sum(
        jnp.where((dp & b) != 0, 1 << (len(bits) - 1 - i), 0) for i, b in enumerate(order)
    )
    own = jnp.concatenate(
        [
            lax.dynamic_slice_in_dim(w_own, place * slab_w, slab_w, 0),
            lax.dynamic_slice_in_dim(gate_rows, place * slab_o, slab_o, 0),
        ],
        axis=0,
    )
    x = jnp.concatenate([x, both], axis=0)
    gain_part = jnp.sum(x[: slab_w + slab_o].astype(F32) * own.astype(F32), axis=0)
    own_slope = jnp.sum(slope_rows, axis=(1, 2))
    chunk = z ^ (c * half)
    slope_part = jnp.where(jnp.arange(n)[:, None] == chunk, own_slope[None, :], 0.0)
    slope_part = jnp.pad(slope_part.reshape(-1), (0, width - n * nh))
    small = jnp.stack([gain_part, slope_part])
    high = small.astype(BF)
    rest = (small - high.astype(F32)).astype(BF)
    x = jnp.concatenate([x, high, rest, jnp.zeros((12, width), BF)], axis=0)
    x = x.reshape([1] * len(bits) + list(x.shape))

    def double_pair(pair, k):
        return [
            double_bit(pair[0], back[k], order.index(back[k])),
            double_bit(pair[1], forth[k], order.index(forth[k])),
        ]

    pair = double_pair([x[..., :side], x[..., side:]], 0)
    pair, moved, cuts = barrier((pair, moved, cuts))
    moved.append(z_swap(cuts[3], half))
    for k in range(1, len(forth)):
        pair = double_pair(pair, k)
    pair, moved = barrier((pair, moved))
    away = jnp.concatenate(moved, axis=0)
    keep = jnp.where(is_home, home, away)
    got = core_swap(jnp.where(is_home, away, home))
    d_normed = jnp.concatenate(
        [jnp.where(c == 0, keep, got), jnp.where(c == 0, got, keep)], axis=0
    ).astype(F32) + d_normed_gate
    pair = [
        double_bit(y, 1, len(bits) - 1).reshape(n_dp, 5 * slab_o + 16, side) for y in pair
    ]
    grad_proj_in, grad_proj_out = assemble(nh, dim, n_dp, width, *pair)
    grad_proj_in = grad_proj_in.reshape(width, nh, 4, dim)
    grad_proj_out = grad_proj_out.reshape(nh, dim, width)

    small = jnp.concatenate([y[:, 5 * slab_o :] for y in pair], axis=-1).astype(F32)
    small = jnp.sum(small, axis=0)
    small = small[:2] + small[2:4]
    step = 1
    while step < n:
        small = small + z_swap(small, step)
        step *= 2
    norm_gain_gradient = small[0] / input_norm_gain
    grad_slope = lax.dynamic_slice_in_dim(small[1], z * nh, nh, 0)

    dh = d_normed * input_norm_gain
    token_gradient = cotangent.astype(F32) + inverse_deviation * (
        dh
        - jnp.mean(dh, axis=1, keepdims=True)
        - xhat * jnp.mean(dh * xhat, axis=1, keepdims=True)
    )
    return (mixed, token_gradient, norm_gain_gradient, grad_proj_in, grad_proj_out, grad_slope)


def solution(mesh):
    return jax.shard_map(
        functools.partial(body, mesh.shape["dp"], mesh.shape["head"]),
        mesh=mesh,
        in_specs=(
            P(("dp", "head"), None),
            P(),
            P(None, "head", None, None),
            P("head", None, None),
            P("head"),
            P("dp", None),
            P(("dp", "head"), None),
        ),
        out_specs=(
            P(("dp", "head"), None),
            P(("dp", "head"), None),
            P(),
            P(None, "head", None, None),
            P("head", None, None),
            P("head"),
        ),
        check_vma=False,
    )
```

```python
import functools

import jax
import jax.numpy as jnp
from jax import lax
from jax.experimental import pallas as pl
from jax.experimental.pallas import tpu as pltpu
from jax.sharding import PartitionSpec as P

EPSILON = 1e-05
BF = jnp.bfloat16
F32 = jnp.float32
AXES = ("dp", "head")
NT = (((1,), (1,)), ((), ()))
TN = (((0,), (0,)), ((), ()))
NN = (((1,), (0,)), ((), ()))


def dot(a, b, dims=NN):
    return lax.dot_general(a, b, dims, preferred_element_type=F32)


def silu_slope(values):
    sigma = jax.nn.sigmoid(values)
    return sigma * (1.0 + values * (1.0 - sigma))


def tanh_slope(values):
    sigma = 0.5 + 0.5 * jnp.tanh(0.5 * values)
    return sigma * (1.0 + values * (1.0 - sigma))


def fill_distance(dist, blocks, rows):
    row = lax.broadcasted_iota(jnp.int32, (rows, rows), 0)
    column = lax.broadcasted_iota(jnp.int32, (rows, rows), 1)

    def one(step, carry):
        offset = jnp.maximum(step * rows + row - column, 0).astype(F32)
        dist[step] = jnp.log(1.0 + offset)
        return carry

    lax.fori_loop(0, blocks, one, 0)


def half_score(q, k, slope, distance, visible, scale):
    u = dot(q, k, NT) * (0.5 * scale) + (0.5 * slope) * distance
    return jnp.where(visible, u, -1.0e4)


def visible_pairs(starts_ref, i, j, rows):
    row = lax.broadcasted_iota(jnp.int32, (rows, rows), 0) + i * rows
    column = lax.broadcasted_iota(jnp.int32, (rows, rows), 1) + j * rows
    first = starts_ref[pl.ds(pl.multiple_of(i * rows, rows), rows), :]
    return (column >= first) & (column <= row)


def forward_kernel(
    nh, dim, rows, blocks, low, held, sent, slopes, starts_ref, w_ref, *refs
):
    pieces = refs[:blocks]
    out_ref, act_hbm, pre_hbm, dist, acc, act_ref, pre_ref, sems = refs[blocks:]
    for b in range(blocks):
        pre = dot(pieces[b][...], w_ref[...], NT)
        half = 0.5 * pre
        pre_ref[b * rows : (b + 1) * rows, :] = pre.astype(BF)
        act_ref[b * rows : (b + 1) * rows, :] = (half + half * jnp.tanh(half)).astype(BF)
    act_copy = pltpu.make_async_copy(act_ref, act_hbm, sems.at[0])
    pre_copy = pltpu.make_async_copy(pre_ref, pre_hbm, sems.at[1])
    act_copy.start()
    pre_copy.start()
    fill_distance(dist, blocks, rows)
    scale = dim ** (-0.5)
    part = nh * dim

    def at(block):
        return pl.ds(pl.multiple_of(block * rows, rows), rows)

    def query_block(i, carry):
        acc[...] = jnp.zeros_like(acc)

        def key_block(j, inner):
            visible = visible_pairs(starts_ref, i, j, rows)
            distance = dist[i - j]
            for h in range(nh):
                q = act_ref[at(held[i]), part + h * dim : part + (h + 1) * dim]
                k = act_ref[at(held[j]), 2 * part + h * dim : 2 * part + (h + 1) * dim]
                v = act_ref[at(held[j]), h * dim : (h + 1) * dim]
                u = half_score(q, k, slopes[h], distance, visible, scale)
                w = (u + u * jnp.tanh(u)).astype(BF)
                acc[:, h * dim : (h + 1) * dim] += dot(w, v)
            return inner

        lax.fori_loop(low[i], i + 1, key_block, 0)
        out_ref[at(sent[i]), :] = acc[...].astype(BF)
        return carry

    lax.fori_loop(0, blocks, query_block, 0)
    act_copy.wait()
    pre_copy.wait()


def backward_kernel(
    nh, dim, rows, blocks, low, held, sent, slopes, starts_ref, act_ref, pre_ref, datt_ref,
    out_ref, slope_ref, dist, dq, dk, dv, gs
):
    fill_distance(dist, blocks, rows)
    scale = dim ** (-0.5)
    part = nh * dim
    dk[...] = jnp.zeros_like(dk)
    dv[...] = jnp.zeros_like(dv)
    gs[...] = jnp.zeros_like(gs)

    def at(block):
        return pl.ds(pl.multiple_of(block * rows, rows), rows)

    def query_block(i, carry):
        dq[...] = jnp.zeros_like(dq)
        mine = held[i]

        def key_block(j, inner):
            visible = visible_pairs(starts_ref, i, j, rows)
            distance = dist[i - j]
            theirs = held[j]
            for h in range(nh):
                cols = slice(h * dim, (h + 1) * dim)
                q = act_ref[at(mine), part + h * dim : part + (h + 1) * dim]
                k = act_ref[at(theirs), 2 * part + h * dim : 2 * part + (h + 1) * dim]
                v = act_ref[at(theirs), cols]
                da = datt_ref[at(sent[i]), cols]
                u = half_score(q, k, slopes[h], distance, visible, scale)
                t = jnp.tanh(u)
                w = u + u * t
                ds = dot(da, v, NT) * ((1.0 + t) + w * (1.0 - t))
                gs[h] += jnp.sum((ds * distance).reshape(rows // 8, 8, rows), axis=0)
                wb = w.astype(BF)
                db = ds.astype(BF)
                dv[at(theirs), cols] += dot(wb, da, TN)
                dk[at(theirs), cols] += dot(db, q, TN)
                dq[:, cols] += dot(db, k)
            return inner

        lax.fori_loop(low[i], i + 1, key_block, 0)
        slope = tanh_slope(pre_ref[at(mine), part : 2 * part].astype(F32))
        out_ref[at(mine), part : 2 * part] = (dq[...] * (0.5 * scale) * slope).astype(BF)
        return carry

    lax.fori_loop(0, blocks, query_block, 0)

    def finish(b, carry):
        slope_v = tanh_slope(pre_ref[at(b), :part].astype(F32))
        out_ref[at(b), :part] = (dv[at(b), :] * slope_v).astype(BF)
        slope_k = tanh_slope(pre_ref[at(b), 2 * part :].astype(F32))
        out_ref[at(b), 2 * part :] = (dk[at(b), :] * (0.5 * scale) * slope_k).astype(BF)
        return carry

    lax.fori_loop(0, blocks, finish, 0)
    for h in range(nh):
        slope_ref[h] = 0.5 * gs[h]


def attention_cost(nh, dim, total, matmuls):
    pairs = total * total // 5
    return pl.CostEstimate(
        flops=30 * matmuls * nh * dim * pairs,
        bytes_accessed=total * nh * dim * 2 * 2 * matmuls,
        transcendentals=nh * pairs,
    )


def attend(nh, dim, rows, tables, slopes, starts, w, pieces):
    blocks = len(pieces)
    total = blocks * rows
    wide = jax.ShapeDtypeStruct((total, 3 * nh * dim), BF)
    smem = pl.BlockSpec(memory_space=pltpu.SMEM)
    vmem = pl.BlockSpec(memory_space=pltpu.VMEM)
    return pl.pallas_call(
        functools.partial(forward_kernel, nh, dim, rows, blocks),
        out_shape=(jax.ShapeDtypeStruct((total, nh * dim), BF), wide, wide),
        in_specs=[smem] * 4 + [vmem] * (2 + blocks),
        out_specs=(vmem,) + (pl.BlockSpec(memory_space=pl.ANY),) * 2,
        scratch_shapes=[
            pltpu.VMEM((blocks, rows, rows), F32),
            pltpu.VMEM((rows, nh * dim), F32),
            pltpu.VMEM(wide.shape, BF),
            pltpu.VMEM(wide.shape, BF),
            pltpu.SemaphoreType.DMA((2,)),
        ],
        compiler_params=pltpu.CompilerParams(vmem_limit_bytes=40 * 2**20),
        cost_estimate=attention_cost(nh, dim, total, 2),
    )(*tables, slopes, starts, w, *pieces)


def unpack_kernel(nh, dim, w_ref, after_ref, own_ref, gate_ref):
    part = nh * dim
    for h in range(nh):
        for kind in range(4):
            x = w_ref[:, h * 4 + kind, :]
            x = x.astype(F32).T.astype(BF)
            at = ((kind - 1) * nh + h) * dim
            if kind:
                own_ref[at : at + dim, :] = x
            else:
                gate_ref[h * dim : (h + 1) * dim, :] = x


def unpack(nh, dim, proj_in, after):
    width = proj_in.shape[0]
    vmem = pl.BlockSpec(memory_space=pltpu.VMEM)
    return pl.pallas_call(
        functools.partial(unpack_kernel, nh, dim),
        out_shape=(
            jax.ShapeDtypeStruct((3 * nh * dim, width), BF),
            jax.ShapeDtypeStruct((nh * dim, width), BF),
        ),
        in_specs=[vmem, pl.BlockSpec(memory_space=pl.ANY)],
        out_specs=(vmem,) * 2,
        compiler_params=pltpu.CompilerParams(vmem_limit_bytes=24 * 2**20),
        cost_estimate=pl.CostEstimate(flops=2 * 10**10, bytes_accessed=8 * 2**20, transcendentals=0),
    )(proj_in.reshape(width, nh * 4, dim), after)


def prepare_kernel(
    n, n_dp, slab, z_ref, all_ref, normed_ref, cot_ref, after_ref,
    gate_w_ref, out_w_ref, pre_gate_ref, d_gated_ref
):
    part = n_dp * slab
    for t in range(n):
        q = z_ref[0] ^ t
        for s in range(n_dp):
            at = t * part + s * slab
            gate_w_ref[at : at + slab, :] = all_ref[s, q, 0]
            out_w_ref[at : at + slab, :] = all_ref[s, q, 1]
    for t in range(n):
        at = slice(t * part, (t + 1) * part)
        pre_gate_ref[:, at] = dot(normed_ref[...], gate_w_ref[at, :], NT)
        d_gated_ref[:, at] = dot(cot_ref[...], out_w_ref[at, :], NT)


def prepare(n, n_dp, slab, z, everything, normed, cotangent, after):
    rows, width = normed.shape
    vmem = pl.BlockSpec(memory_space=pltpu.VMEM)
    columns = n * n_dp * slab
    return pl.pallas_call(
        functools.partial(prepare_kernel, n, n_dp, slab),
        out_shape=(
            jax.ShapeDtypeStruct((columns, width), BF),
            jax.ShapeDtypeStruct((columns, width), BF),
            jax.ShapeDtypeStruct((rows, columns), F32),
            jax.ShapeDtypeStruct((rows, columns), F32),
        ),
        in_specs=[pl.BlockSpec(memory_space=pltpu.SMEM)]
        + [vmem] * 3
        + [pl.BlockSpec(memory_space=pl.ANY)],
        out_specs=(vmem,) * 4,
        compiler_params=pltpu.CompilerParams(vmem_limit_bytes=32 * 2**20),
        cost_estimate=pl.CostEstimate(
            flops=20 * rows * width * columns, bytes_accessed=16 * 2**20, transcendentals=0
        ),
    )(z.reshape(1), everything, normed, cotangent, after)


def gate_kernel(n, step, pre_gate_ref, d_gated_ref, normed_ref, cot_ref, *refs):
    pieces, d_att = refs[:n], refs[n : 2 * n]
    both_ref, gated_ref, d_pre_gate_ref, dn_ref = refs[2 * n :]
    rows, width = pre_gate_ref.shape
    part = width // n

    def some_rows(r, carry):
        at = pl.ds(pl.multiple_of(r * step, step), step)
        att = [ref[at, :].astype(F32) for ref in pieces]
        mean = sum(jnp.sum(x, axis=1, keepdims=True) for x in att) / width
        square = sum(jnp.sum(x * x, axis=1, keepdims=True) for x in att) / width
        inv = lax.rsqrt(square - mean * mean + EPSILON)
        first = jnp.zeros((step, 1), F32)
        second = jnp.zeros((step, 1), F32)
        for t in range(n):
            columns = slice(t * part, (t + 1) * part)
            normed_o = (att[t] - mean) * inv
            pre = pre_gate_ref[at, columns]
            d_gated = d_gated_ref[at, columns]
            sigma = 0.5 + 0.5 * jnp.tanh(0.5 * pre)
            gate = (pre * sigma).astype(BF).astype(F32)
            gated_ref[at, columns] = (normed_o * gate).astype(BF)
            dn = d_gated * gate
            first += jnp.sum(dn, axis=1, keepdims=True)
            second += jnp.sum(dn * normed_o, axis=1, keepdims=True)
            d_gate = (d_gated * normed_o).astype(BF).astype(F32)
            slope = sigma * (1.0 + pre * (1.0 - sigma))
            d_pre_gate_ref[at, columns] = (d_gate * slope).astype(BF)
            dn_ref[:, columns] = dn
        first, second = first / width, second / width
        for t in range(n):
            columns = slice(t * part, (t + 1) * part)
            normed_o = (att[t] - mean) * inv
            dn = dn_ref[:, columns]
            d_att[t][at, :] = (inv * (dn - first - normed_o * second)).astype(BF)
        return carry

    lax.fori_loop(0, rows // step, some_rows, 0)
    for t in range(n):
        columns = slice(t * part, (t + 1) * part)
        both_ref[0, columns, :] = dot(d_pre_gate_ref[:, columns], normed_ref[...], TN).astype(BF)
        both_ref[1, columns, :] = dot(gated_ref[:, columns], cot_ref[...], TN).astype(BF)


def gate_and_norm(n, pre_gate, d_gated, normed, cotangent, pieces):
    rows, width = normed.shape
    columns = pre_gate.shape[1]
    vmem = pl.BlockSpec(memory_space=pltpu.VMEM)
    outs = pl.pallas_call(
        functools.partial(gate_kernel, n, 64),
        out_shape=[jax.ShapeDtypeStruct(x.shape, BF) for x in pieces]
        + [
            jax.ShapeDtypeStruct((2, columns, width), BF),
            jax.ShapeDtypeStruct((rows, columns), BF),
            jax.ShapeDtypeStruct((rows, columns), BF),
        ],
        in_specs=[vmem] * (4 + n),
        out_specs=[vmem] * (n + 3),
        scratch_shapes=[pltpu.VMEM((64, columns), F32)],
        compiler_params=pltpu.CompilerParams(vmem_limit_bytes=32 * 2**20),
        cost_estimate=pl.CostEstimate(
            flops=8 * rows * width * columns, bytes_accessed=16 * 2**20, transcendentals=0
        ),
    )(pre_gate, d_gated, normed, cotangent, *pieces)
    return list(outs[:n]), outs[n], outs[n + 1], outs[n + 2]


def assemble_kernel(nh, dim, n_dp, first_ref, second_ref, in_ref, out_ref, rows_ref):
    part = nh * dim
    slab = part // n_dp
    side = first_ref.shape[2]
    for s in range(n_dp):
        for side_at, ref in ((0, first_ref), (1, second_ref)):
            x = ref[s].astype(F32)
            columns = slice(side_at * side, (side_at + 1) * side)
            rows_ref[3 * s * slab : 3 * (s + 1) * slab, columns] = x[: 3 * slab]
            at = 3 * part + s * slab
            rows_ref[at : at + slab, columns] = x[3 * slab : 4 * slab]
            out_ref[s * slab : (s + 1) * slab, columns] = x[4 * slab : 5 * slab]
    for h in range(nh):
        for kind in range(4):
            at = kind * part + h * dim
            in_ref[:, h * 4 + (kind + 1) % 4, :] = rows_ref[at : at + dim, :].T


def assemble(nh, dim, n_dp, width, first, second):
    vmem = pl.BlockSpec(memory_space=pltpu.VMEM)
    return pl.pallas_call(
        functools.partial(assemble_kernel, nh, dim, n_dp),
        out_shape=(
            jax.ShapeDtypeStruct((width, nh * 4, dim), F32),
            jax.ShapeDtypeStruct((nh * dim, width), F32),
        ),
        in_specs=[vmem] * 2,
        out_specs=(vmem,) * 2,
        scratch_shapes=[pltpu.VMEM((4 * nh * dim, width), F32)],
        compiler_params=pltpu.CompilerParams(vmem_limit_bytes=40 * 2**20),
        cost_estimate=pl.CostEstimate(flops=0, bytes_accessed=8 * 2**20, transcendentals=0),
    )(first, second)


def attend_back(nh, dim, rows, tables, slopes, starts, act, pre, d_attended):
    total = act.shape[0]
    blocks = total // rows
    smem = pl.BlockSpec(memory_space=pltpu.SMEM)
    vmem = pl.BlockSpec(memory_space=pltpu.VMEM)
    return pl.pallas_call(
        functools.partial(backward_kernel, nh, dim, rows, blocks),
        out_shape=(
            jax.ShapeDtypeStruct(act.shape, BF),
            jax.ShapeDtypeStruct((nh, 8, rows), F32),
        ),
        in_specs=[smem] * 4 + [vmem] * 4,
        out_specs=(vmem, vmem),
        scratch_shapes=[
            pltpu.VMEM((blocks, rows, rows), F32),
            pltpu.VMEM((rows, nh * dim), F32),
            pltpu.VMEM((total, nh * dim), F32),
            pltpu.VMEM((total, nh * dim), F32),
            pltpu.VMEM((nh, 8, rows), F32),
        ],
        compiler_params=pltpu.CompilerParams(vmem_limit_bytes=48 * 2**20),
        cost_estimate=attention_cost(nh, dim, total, 5),
    )(*tables, slopes, starts, act, pre, d_attended)


def body(
    n_dp, n, tokens, input_norm_gain, proj_in, proj_out, bias_slope, lengths, cotangent
):
    local_rows, width = tokens.shape
    nh, dim = proj_in.shape[1], proj_in.shape[3]
    part = nh * dim
    rows = local_rows // 2
    half = n // 2
    dp = lax.axis_index("dp")
    z = lax.axis_index("head")
    c = dp & 1
    host = (z >= half).astype(jnp.int32)
    is_home = c == host

    def move(x, target):
        pairs = []
        for d in range(n_dp):
            for s in range(n):
                e, t = target(d, s)
                pairs.append((d * n + s, e * n + t))
        return lax.ppermute(x, AXES, pairs)

    def core_swap(x):
        return move(x, lambda d, s: (d ^ 1, s))

    def z_swap(x, bit):
        return move(x, lambda d, s: (d, s ^ bit))

    def dp_swap(x, bit):
        return move(x, lambda d, s: (d ^ bit, s))

    def send_target(r):
        def target(d, s):
            core = int(s >= half)
            return ((d & ~1) | core, s ^ r ^ ((d & 1) * half))

        return target

    def back_target(r):
        forward = {}
        for d in range(n_dp):
            for s in range(n):
                forward[send_target(r)(d, s)] = (d, s)
        return lambda d, s: forward[(d, s)]

    def cross(x):
        return move(x, lambda d, s: (d, s ^ ((d & 1) * half)))

    token_single = tokens.astype(F32)
    centred_input = jnp.mean(token_single, axis=1, keepdims=True)
    spread = jnp.mean((token_single - centred_input) ** 2, axis=1, keepdims=True)
    inverse_deviation = lax.rsqrt(spread + EPSILON)
    xhat = (token_single - centred_input) * inverse_deviation
    normed = (xhat * input_norm_gain).astype(BF)

    first, second = normed[:rows], normed[rows:]
    keep = jnp.where(c == 0, first, second)
    give = jnp.where(c == 0, second, first)
    barrier = lax.optimization_barrier
    bits = [1 << b for b in range(n_dp.bit_length() - 1)]
    slab_o = part // n_dp
    slab_w = 3 * slab_o
    got = core_swap(give)
    w_own, gate_rows = unpack(nh, dim, proj_in, give)
    mirrored = sum(
        jnp.where((dp & b) != 0, bits[-1] // b, 0) for b in bits
    )
    w_slab = lax.dynamic_slice_in_dim(w_own, mirrored * slab_w, slab_w, 0)
    items = {0: jnp.where(is_home, keep, got)}
    crossed = z_swap(
        jnp.concatenate([jnp.where(is_home, got, keep), w_slab], axis=0), half
    )
    bit = 1
    while bit < half:
        for t in sorted(items):
            items[t ^ bit] = z_swap(items[t], bit)
        bit *= 2
    own_lengths = lengths[0]
    hosted_lengths = jnp.where(is_home, own_lengths, core_swap(own_lengths))
    total = n * local_rows
    ends = jnp.cumsum(hosted_lengths)
    positions = jnp.arange(total, dtype=jnp.int32)
    starts = jnp.max(
        jnp.where(positions[:, None] >= ends[None, :], ends[None, :], 0), axis=1, keepdims=True
    ).astype(jnp.int32)
    block = jnp.arange(total // rows, dtype=jnp.int32)
    low = starts[::rows, 0] // rows
    shard = (block // 2) ^ z
    held = ((block & 1) ^ c) * n + shard
    sent = 2 * (shard ^ (c * half)) + (block & 1)
    tables = (low, held, sent)
    slopes = cross(bias_slope)

    items, crossed, tables, starts, slopes = barrier((items, crossed, tables, starts, slopes))
    piece = crossed[rows:]

    def dp_double(x, bit):
        other = dp_swap(x, bit)
        up = (dp & bit) != 0
        return jnp.concatenate([jnp.where(up, other, x), jnp.where(up, x, other)], axis=0)

    def spread(x):
        found = {half: x}
        bit = 1
        while bit < half:
            for t in sorted(found):
                found[t ^ bit] = z_swap(found[t], bit)
            bit *= 2
        return found

    middle = rows // 2
    upper = spread(crossed[:middle])
    for b in bits[:1:-1]:
        piece = dp_double(piece, b)
    upper, piece, lower = barrier((upper, piece, crossed[middle:rows]))
    lower = spread(lower)
    piece = dp_double(piece, bits[1])
    items, upper, lower, piece = barrier((items, upper, lower, piece))
    piece = dp_double(piece, bits[0])
    for t in upper:
        items[t] = jnp.concatenate([upper[t], lower[t]], axis=0)
    mine = [items[t] for t in range(n)]
    theirs = [core_swap(x) for x in mine]

    slabs = jnp.concatenate(
        [
            lax.dynamic_slice_in_dim(gate_rows, dp * slab_o, slab_o, 0),
            lax.dynamic_slice_in_dim(proj_out.reshape(part, width), dp * slab_o, slab_o, 0),
        ],
        axis=0,
    )
    everything = lax.all_gather(slabs, AXES).reshape(n_dp, n, 2, slab_o, width)

    w_qkv = jnp.where(c == 0, w_own, piece)

    attended, act, pre = attend(
        nh, dim, rows, tables, slopes, starts, w_qkv, mine + theirs
    )
    w_gate, w_out, pre_gate, d_gated = prepare(
        n, n_dp, slab_o, z, everything, normed, cotangent, attended
    )
    gathered = jnp.concatenate(mine + theirs, axis=0)
    arrived = [
        move(attended[r * local_rows : (r + 1) * local_rows], send_target(r)) for r in range(n)
    ]
    arrived, w_gate, w_out, pre_gate, d_gated = barrier(
        (arrived, w_gate, w_out, pre_gate, d_gated)
    )
    d_attended, both, gated, d_pre_gate = gate_and_norm(
        n, pre_gate, d_gated, normed, cotangent, arrived
    )

    def add(x, y):
        return (x.astype(F32) + y.astype(F32)).astype(BF)

    order = bits[1:] + bits[:1]
    split = [2] * len(bits)
    forth, back = bits[1:], bits[:0:-1]

    def reduce_bit(x, b, axis):
        up = (dp & b) != 0
        low_half = lax.slice_in_dim(x, 0, 1, axis=axis)
        high_half = lax.slice_in_dim(x, 1, 2, axis=axis)
        return add(
            jnp.where(up, high_half, low_half),
            dp_swap(jnp.where(up, low_half, high_half), b),
        )

    def double_bit(x, b, axis):
        other = dp_swap(x, b)
        up = (dp & b) != 0
        return jnp.concatenate(
            [jnp.where(up, other, x), jnp.where(up, x, other)], axis=axis
        )

    both = both.reshape([2, n] + split + [slab_o, width])
    both = reduce_bit(both, 1, 1 + len(bits))
    arrived = [
        move(d_attended[r], back_target(r)) for r in range(n)
    ]
    d_att = jnp.concatenate(arrived, axis=0)
    pair = [both[0], both[1]]
    def reduce_pair(pair, k, first_axis):
        return [
            reduce_bit(pair[0], forth[k], first_axis + order.index(forth[k])),
            reduce_bit(pair[1], back[k], first_axis + order.index(back[k])),
        ]

    both = reduce_pair(pair, 0, 1)
    mixed = (token_single + dot(gated, w_out)).astype(BF)
    d_normed_gate = dot(d_pre_gate, w_gate)
    d_att, both, mixed, d_normed_gate = barrier((d_att, both, mixed, d_normed_gate))
    for k in range(1, len(forth)):
        both = reduce_pair(both, k, 1)

    d_pre, slope_rows = attend_back(
        nh, dim, rows, tables, slopes, starts, act, pre, d_att
    )

    def partial(first_block, last_block):
        return dot(d_pre[first_block * rows : last_block * rows], w_qkv).astype(BF)

    d_pre, both = barrier((d_pre, both))
    theirs = partial(n, 2 * n)
    got = core_swap(theirs)
    d_pre, theirs = barrier((d_pre, theirs))
    in_part = dot(d_pre, gathered, TN).astype(BF)
    mine = partial(0, n)
    both = jnp.stack(both).reshape(2, n, slab_o, width)
    both = add(both[:, :half], z_swap(both[:, half:], half))
    in_part, got, both = barrier((in_part, got, both))

    side = width // 2
    x = in_part.reshape(split + [slab_w, width])
    pair = reduce_pair([x[..., :side], x[..., side:]], 0, 0)
    home, away = add(mine[: half * rows], got[: half * rows]), add(
        mine[half * rows :], got[half * rows :]
    )
    bit = half // 2
    while bit >= 1:
        away = add(away[: bit * rows], z_swap(away[bit * rows :], bit))
        bit //= 2
    bit = half // 2
    while bit >= 1:
        both = add(both[:, :bit], z_swap(both[:, bit:], bit))
        bit //= 2
    both = both.reshape(2 * slab_o, width)
    for k in range(1, len(forth)):
        pair = reduce_pair(pair, k, 0)
    pair, away, home, both = barrier((pair, away, home, both))

    cuts = [away[k * rows // 4 : (k + 1) * rows // 4] for k in range(4)]
    moved = [z_swap(cuts[0], half)]
    x = cross(jnp.concatenate(pair, axis=-1))
    x, moved, home, both, cuts = barrier((x, moved, home, both, cuts))

    moved.append(z_swap(cuts[1], half))
    x = reduce_bit(x, 1, len(bits) - 1)
    bit = half // 2
    while bit > 1:
        home = add(home[: bit * rows], z_swap(home[bit * rows :], bit))
        bit //= 2
    homes = [home[:middle]]
    if bit:
        homes[0] = add(homes[0], z_swap(home[rows : rows + middle], 1))
    x, moved, cuts, homes, home = barrier((x, moved, cuts, homes, home))
    homes.append(home[middle:rows])
    if bit:
        homes[1] = add(homes[1], z_swap(home[rows + middle :], 1))
    moved.append(z_swap(cuts[2], half))
    x = x.reshape(slab_w, width)
    place = sum(
        jnp.where((dp & b) != 0, 1 << (len(bits) - 1 - i), 0) for i, b in enumerate(order)
    )
    own = jnp.concatenate(
        [
            lax.dynamic_slice_in_dim(w_own, place * slab_w, slab_w, 0),
            lax.dynamic_slice_in_dim(gate_rows, place * slab_o, slab_o, 0),
        ],
        axis=0,
    )
    x = jnp.concatenate([x, both], axis=0)
    gain_part = jnp.sum(x[: slab_w + slab_o].astype(F32) * own.astype(F32), axis=0)
    own_slope = jnp.sum(slope_rows, axis=(1, 2))
    chunk = z ^ (c * half)
    slope_part = jnp.where(jnp.arange(n)[:, None] == chunk, own_slope[None, :], 0.0)
    slope_part = jnp.pad(slope_part.reshape(-1), (0, width - n * nh))
    small = jnp.stack([gain_part, slope_part])
    high = small.astype(BF)
    rest = (small - high.astype(F32)).astype(BF)
    x = jnp.concatenate([x, high, rest, jnp.zeros((12, width), BF)], axis=0)
    x = x.reshape([1] * len(bits) + list(x.shape))

    def double_pair(pair, k):
        return [
            double_bit(pair[0], back[k], order.index(back[k])),
            double_bit(pair[1], forth[k], order.index(forth[k])),
        ]

    pair = double_pair([x[..., :side], x[..., side:]], 0)
    pair, moved, cuts, homes = barrier((pair, moved, cuts, homes))
    home = jnp.concatenate(homes, axis=0)
    moved.append(z_swap(cuts[3], half))
    for k in range(1, len(forth)):
        pair = double_pair(pair, k)
    pair, moved = barrier((pair, moved))
    away = jnp.concatenate(moved, axis=0)
    keep = jnp.where(is_home, home, away)
    got = core_swap(jnp.where(is_home, away, home))
    d_normed = jnp.concatenate(
        [jnp.where(c == 0, keep, got), jnp.where(c == 0, got, keep)], axis=0
    ).astype(F32) + d_normed_gate
    pair = [
        double_bit(y, 1, len(bits) - 1).reshape(n_dp, 5 * slab_o + 16, side) for y in pair
    ]
    grad_proj_in, grad_proj_out = assemble(nh, dim, n_dp, width, *pair)
    grad_proj_in = grad_proj_in.reshape(width, nh, 4, dim)
    grad_proj_out = grad_proj_out.reshape(nh, dim, width)

    small = jnp.concatenate([y[:, 5 * slab_o :] for y in pair], axis=-1).astype(F32)
    small = jnp.sum(small, axis=0)
    small = small[:2] + small[2:4]
    step = 1
    while step < n:
        small = small + z_swap(small, step)
        step *= 2
    norm_gain_gradient = small[0] / input_norm_gain
    grad_slope = lax.dynamic_slice_in_dim(small[1], z * nh, nh, 0)

    dh = d_normed * input_norm_gain
    token_gradient = cotangent.astype(F32) + inverse_deviation * (
        dh
        - jnp.mean(dh, axis=1, keepdims=True)
        - xhat * jnp.mean(dh * xhat, axis=1, keepdims=True)
    )
    return (mixed, token_gradient, norm_gain_gradient, grad_proj_in, grad_proj_out, grad_slope)


def solution(mesh):
    return jax.shard_map(
        functools.partial(body, mesh.shape["dp"], mesh.shape["head"]),
        mesh=mesh,
        in_specs=(
            P(("dp", "head"), None),
            P(),
            P(None, "head", None, None),
            P("head", None, None),
            P("head"),
            P("dp", None),
            P(("dp", "head"), None),
        ),
        out_specs=(
            P(("dp", "head"), None),
            P(("dp", "head"), None),
            P(),
            P(None, "head", None, None),
            P("head", None, None),
            P("head"),
        ),
        check_vma=False,
    )
```

```python
import functools

import jax
import jax.numpy as jnp
from jax import lax
from jax.experimental import pallas as pl
from jax.experimental.pallas import tpu as pltpu
from jax.sharding import PartitionSpec as P

EPSILON = 1e-05
BF = jnp.bfloat16
F32 = jnp.float32
AXES = ("dp", "head")
NT = (((1,), (1,)), ((), ()))
TN = (((0,), (0,)), ((), ()))
NN = (((1,), (0,)), ((), ()))


def dot(a, b, dims=NN):
    return lax.dot_general(a, b, dims, preferred_element_type=F32)


def silu_slope(values):
    sigma = jax.nn.sigmoid(values)
    return sigma * (1.0 + values * (1.0 - sigma))


def tanh_slope(values):
    sigma = 0.5 + 0.5 * jnp.tanh(0.5 * values)
    return sigma * (1.0 + values * (1.0 - sigma))


def fill_distance(dist, blocks, rows):
    row = lax.broadcasted_iota(jnp.int32, (rows, rows), 0)
    column = lax.broadcasted_iota(jnp.int32, (rows, rows), 1)

    def one(step, carry):
        offset = jnp.maximum(step * rows + row - column, 0).astype(F32)
        dist[step] = jnp.log(1.0 + offset)
        return carry

    lax.fori_loop(0, blocks, one, 0)


def half_score(q, k, slope, distance, visible, scale):
    u = dot(q, k, NT) * (0.5 * scale) + (0.5 * slope) * distance
    return jnp.where(visible, u, -1.0e4)


def visible_pairs(starts_ref, i, j, rows):
    row = lax.broadcasted_iota(jnp.int32, (rows, rows), 0) + i * rows
    column = lax.broadcasted_iota(jnp.int32, (rows, rows), 1) + j * rows
    first = starts_ref[pl.ds(pl.multiple_of(i * rows, rows), rows), :]
    return (column >= first) & (column <= row)


def forward_kernel(
    nh, dim, rows, blocks, low, held, sent, slopes, starts_ref, w_ref, *refs
):
    pieces = refs[:blocks]
    out_ref, act_hbm, pre_hbm, dist, acc, act_ref, pre_ref, sems = refs[blocks:]
    for b in range(blocks):
        pre = dot(pieces[b][...], w_ref[...], NT)
        half = 0.5 * pre
        pre_ref[b * rows : (b + 1) * rows, :] = pre.astype(BF)
        act_ref[b * rows : (b + 1) * rows, :] = (half + half * jnp.tanh(half)).astype(BF)
    act_copy = pltpu.make_async_copy(act_ref, act_hbm, sems.at[0])
    pre_copy = pltpu.make_async_copy(pre_ref, pre_hbm, sems.at[1])
    act_copy.start()
    pre_copy.start()
    fill_distance(dist, blocks, rows)
    scale = dim ** (-0.5)
    part = nh * dim

    def at(block):
        return pl.ds(pl.multiple_of(block * rows, rows), rows)

    def query_block(i, carry):
        acc[...] = jnp.zeros_like(acc)

        def key_block(j, inner):
            visible = visible_pairs(starts_ref, i, j, rows)
            distance = dist[i - j]
            for h in range(nh):
                q = act_ref[at(held[i]), part + h * dim : part + (h + 1) * dim]
                k = act_ref[at(held[j]), 2 * part + h * dim : 2 * part + (h + 1) * dim]
                v = act_ref[at(held[j]), h * dim : (h + 1) * dim]
                u = half_score(q, k, slopes[h], distance, visible, scale)
                w = (u + u * jnp.tanh(u)).astype(BF)
                acc[:, h * dim : (h + 1) * dim] += dot(w, v)
            return inner

        lax.fori_loop(low[i], i + 1, key_block, 0)
        out_ref[at(sent[i]), :] = acc[...].astype(BF)
        return carry

    lax.fori_loop(0, blocks, query_block, 0)
    act_copy.wait()
    pre_copy.wait()


def backward_kernel(
    nh, dim, rows, blocks, low, held, sent, slopes, starts_ref, act_ref, pre_ref, datt_ref,
    out_ref, slope_ref, dist, dq, dk, dv, gs
):
    fill_distance(dist, blocks, rows)
    scale = dim ** (-0.5)
    part = nh * dim
    dk[...] = jnp.zeros_like(dk)
    dv[...] = jnp.zeros_like(dv)
    gs[...] = jnp.zeros_like(gs)

    def at(block):
        return pl.ds(pl.multiple_of(block * rows, rows), rows)

    def query_block(i, carry):
        dq[...] = jnp.zeros_like(dq)
        mine = held[i]

        def key_block(j, inner):
            visible = visible_pairs(starts_ref, i, j, rows)
            distance = dist[i - j]
            theirs = held[j]
            for h in range(nh):
                cols = slice(h * dim, (h + 1) * dim)
                q = act_ref[at(mine), part + h * dim : part + (h + 1) * dim]
                k = act_ref[at(theirs), 2 * part + h * dim : 2 * part + (h + 1) * dim]
                v = act_ref[at(theirs), cols]
                da = datt_ref[at(sent[i]), cols]
                u = half_score(q, k, slopes[h], distance, visible, scale)
                t = jnp.tanh(u)
                w = u + u * t
                ds = dot(da, v, NT) * ((1.0 + t) + w * (1.0 - t))
                gs[h] += jnp.sum((ds * distance).reshape(rows // 8, 8, rows), axis=0)
                wb = w.astype(BF)
                db = ds.astype(BF)
                dv[at(theirs), cols] += dot(wb, da, TN)
                dk[at(theirs), cols] += dot(db, q, TN)
                dq[:, cols] += dot(db, k)
            return inner

        lax.fori_loop(low[i], i + 1, key_block, 0)
        slope = tanh_slope(pre_ref[at(mine), part : 2 * part].astype(F32))
        out_ref[at(mine), part : 2 * part] = (dq[...] * (0.5 * scale) * slope).astype(BF)
        return carry

    lax.fori_loop(0, blocks, query_block, 0)

    def finish(b, carry):
        slope_v = tanh_slope(pre_ref[at(b), :part].astype(F32))
        out_ref[at(b), :part] = (dv[at(b), :] * slope_v).astype(BF)
        slope_k = tanh_slope(pre_ref[at(b), 2 * part :].astype(F32))
        out_ref[at(b), 2 * part :] = (dk[at(b), :] * (0.5 * scale) * slope_k).astype(BF)
        return carry

    lax.fori_loop(0, blocks, finish, 0)
    for h in range(nh):
        slope_ref[h] = 0.5 * gs[h]


def attention_cost(nh, dim, total, matmuls):
    pairs = total * total // 5
    return pl.CostEstimate(
        flops=30 * matmuls * nh * dim * pairs,
        bytes_accessed=total * nh * dim * 2 * 2 * matmuls,
        transcendentals=nh * pairs,
    )


def attend(nh, dim, rows, tables, slopes, starts, w, pieces):
    blocks = len(pieces)
    total = blocks * rows
    wide = jax.ShapeDtypeStruct((total, 3 * nh * dim), BF)
    smem = pl.BlockSpec(memory_space=pltpu.SMEM)
    vmem = pl.BlockSpec(memory_space=pltpu.VMEM)
    return pl.pallas_call(
        functools.partial(forward_kernel, nh, dim, rows, blocks),
        out_shape=(jax.ShapeDtypeStruct((total, nh * dim), BF), wide, wide),
        in_specs=[smem] * 4 + [vmem] * (2 + blocks),
        out_specs=(vmem,) + (pl.BlockSpec(memory_space=pltpu.HBM),) * 2,
        scratch_shapes=[
            pltpu.VMEM((blocks, rows, rows), F32),
            pltpu.VMEM((rows, nh * dim), F32),
            pltpu.VMEM(wide.shape, BF),
            pltpu.VMEM(wide.shape, BF),
            pltpu.SemaphoreType.DMA((2,)),
        ],
        compiler_params=pltpu.CompilerParams(vmem_limit_bytes=40 * 2**20),
        cost_estimate=attention_cost(nh, dim, total, 2),
    )(*tables, slopes, starts, w, *pieces)


def unpack_kernel(nh, dim, w_ref, after_ref, own_ref, gate_ref):
    part = nh * dim
    for h in range(nh):
        for kind in range(4):
            x = w_ref[:, h * 4 + kind, :]
            x = x.astype(F32).T.astype(BF)
            at = ((kind - 1) * nh + h) * dim
            if kind:
                own_ref[at : at + dim, :] = x
            else:
                gate_ref[h * dim : (h + 1) * dim, :] = x


def unpack(nh, dim, proj_in, after):
    width = proj_in.shape[0]
    vmem = pl.BlockSpec(memory_space=pltpu.VMEM)
    return pl.pallas_call(
        functools.partial(unpack_kernel, nh, dim),
        out_shape=(
            jax.ShapeDtypeStruct((3 * nh * dim, width), BF),
            jax.ShapeDtypeStruct((nh * dim, width), BF),
        ),
        in_specs=[vmem, pl.BlockSpec(memory_space=pl.ANY)],
        out_specs=(vmem,) * 2,
        compiler_params=pltpu.CompilerParams(vmem_limit_bytes=24 * 2**20),
        cost_estimate=pl.CostEstimate(flops=2 * 10**10, bytes_accessed=8 * 2**20, transcendentals=0),
    )(proj_in.reshape(width, nh * 4, dim), after)


def prepare_kernel(
    n, n_dp, slab, z_ref, all_ref, normed_ref, cot_ref, after_ref,
    gate_w_ref, out_w_ref, pre_gate_ref, d_gated_ref
):
    part = n_dp * slab
    for t in range(n):
        q = z_ref[0] ^ t
        for s in range(n_dp):
            at = t * part + s * slab
            gate_w_ref[at : at + slab, :] = all_ref[s, q, 0]
            out_w_ref[at : at + slab, :] = all_ref[s, q, 1]
    for t in range(n):
        at = slice(t * part, (t + 1) * part)
        pre_gate_ref[:, at] = dot(normed_ref[...], gate_w_ref[at, :], NT)
        d_gated_ref[:, at] = dot(cot_ref[...], out_w_ref[at, :], NT)


def prepare(n, n_dp, slab, z, everything, normed, cotangent, after):
    rows, width = normed.shape
    vmem = pl.BlockSpec(memory_space=pltpu.VMEM)
    columns = n * n_dp * slab
    return pl.pallas_call(
        functools.partial(prepare_kernel, n, n_dp, slab),
        out_shape=(
            jax.ShapeDtypeStruct((columns, width), BF),
            jax.ShapeDtypeStruct((columns, width), BF),
            jax.ShapeDtypeStruct((rows, columns), F32),
            jax.ShapeDtypeStruct((rows, columns), F32),
        ),
        in_specs=[pl.BlockSpec(memory_space=pltpu.SMEM)]
        + [vmem] * 3
        + [pl.BlockSpec(memory_space=pl.ANY)],
        out_specs=(vmem,) * 4,
        compiler_params=pltpu.CompilerParams(vmem_limit_bytes=32 * 2**20),
        cost_estimate=pl.CostEstimate(
            flops=20 * rows * width * columns, bytes_accessed=16 * 2**20, transcendentals=0
        ),
    )(z.reshape(1), everything, normed, cotangent, after)


def gate_kernel(n, step, pre_gate_ref, d_gated_ref, normed_ref, cot_ref, *refs):
    pieces, d_att = refs[:n], refs[n : 2 * n]
    both_ref, gated_ref, d_pre_gate_ref, dn_ref = refs[2 * n :]
    rows, width = pre_gate_ref.shape
    part = width // n

    def some_rows(r, carry):
        at = pl.ds(pl.multiple_of(r * step, step), step)
        att = [ref[at, :].astype(F32) for ref in pieces]
        mean = sum(jnp.sum(x, axis=1, keepdims=True) for x in att) / width
        square = sum(jnp.sum(x * x, axis=1, keepdims=True) for x in att) / width
        inv = lax.rsqrt(square - mean * mean + EPSILON)
        first = jnp.zeros((step, 1), F32)
        second = jnp.zeros((step, 1), F32)
        for t in range(n):
            columns = slice(t * part, (t + 1) * part)
            normed_o = (att[t] - mean) * inv
            pre = pre_gate_ref[at, columns]
            d_gated = d_gated_ref[at, columns]
            sigma = 0.5 + 0.5 * jnp.tanh(0.5 * pre)
            gate = (pre * sigma).astype(BF).astype(F32)
            gated_ref[at, columns] = (normed_o * gate).astype(BF)
            dn = d_gated * gate
            first += jnp.sum(dn, axis=1, keepdims=True)
            second += jnp.sum(dn * normed_o, axis=1, keepdims=True)
            d_gate = (d_gated * normed_o).astype(BF).astype(F32)
            slope = sigma * (1.0 + pre * (1.0 - sigma))
            d_pre_gate_ref[at, columns] = (d_gate * slope).astype(BF)
            dn_ref[:, columns] = dn
        first, second = first / width, second / width
        for t in range(n):
            columns = slice(t * part, (t + 1) * part)
            normed_o = (att[t] - mean) * inv
            dn = dn_ref[:, columns]
            d_att[t][at, :] = (inv * (dn - first - normed_o * second)).astype(BF)
        return carry

    lax.fori_loop(0, rows // step, some_rows, 0)
    for t in range(n):
        columns = slice(t * part, (t + 1) * part)
        both_ref[0, columns, :] = dot(d_pre_gate_ref[:, columns], normed_ref[...], TN).astype(BF)
        both_ref[1, columns, :] = dot(gated_ref[:, columns], cot_ref[...], TN).astype(BF)


def gate_and_norm(n, pre_gate, d_gated, normed, cotangent, pieces):
    rows, width = normed.shape
    columns = pre_gate.shape[1]
    vmem = pl.BlockSpec(memory_space=pltpu.VMEM)
    outs = pl.pallas_call(
        functools.partial(gate_kernel, n, 64),
        out_shape=[jax.ShapeDtypeStruct(x.shape, BF) for x in pieces]
        + [
            jax.ShapeDtypeStruct((2, columns, width), BF),
            jax.ShapeDtypeStruct((rows, columns), BF),
            jax.ShapeDtypeStruct((rows, columns), BF),
        ],
        in_specs=[vmem] * (4 + n),
        out_specs=[vmem] * (n + 3),
        scratch_shapes=[pltpu.VMEM((64, columns), F32)],
        compiler_params=pltpu.CompilerParams(vmem_limit_bytes=32 * 2**20),
        cost_estimate=pl.CostEstimate(
            flops=8 * rows * width * columns, bytes_accessed=16 * 2**20, transcendentals=0
        ),
    )(pre_gate, d_gated, normed, cotangent, *pieces)
    return list(outs[:n]), outs[n], outs[n + 1], outs[n + 2]


def assemble_kernel(nh, dim, n_dp, first_ref, second_ref, in_ref, out_ref, rows_ref):
    part = nh * dim
    slab = part // n_dp
    side = first_ref.shape[2]
    for s in range(n_dp):
        for side_at, ref in ((0, first_ref), (1, second_ref)):
            x = ref[s].astype(F32)
            columns = slice(side_at * side, (side_at + 1) * side)
            rows_ref[3 * s * slab : 3 * (s + 1) * slab, columns] = x[: 3 * slab]
            at = 3 * part + s * slab
            rows_ref[at : at + slab, columns] = x[3 * slab : 4 * slab]
            out_ref[s * slab : (s + 1) * slab, columns] = x[4 * slab : 5 * slab]
    for h in range(nh):
        for kind in range(4):
            at = kind * part + h * dim
            in_ref[:, h * 4 + (kind + 1) % 4, :] = rows_ref[at : at + dim, :].T


def assemble(nh, dim, n_dp, width, first, second):
    vmem = pl.BlockSpec(memory_space=pltpu.VMEM)
    return pl.pallas_call(
        functools.partial(assemble_kernel, nh, dim, n_dp),
        out_shape=(
            jax.ShapeDtypeStruct((width, nh * 4, dim), F32),
            jax.ShapeDtypeStruct((nh * dim, width), F32),
        ),
        in_specs=[vmem] * 2,
        out_specs=(vmem,) * 2,
        scratch_shapes=[pltpu.VMEM((4 * nh * dim, width), F32)],
        compiler_params=pltpu.CompilerParams(vmem_limit_bytes=40 * 2**20),
        cost_estimate=pl.CostEstimate(
            flops=10**10, bytes_accessed=8 * 2**20, transcendentals=0
        ),
    )(first, second)


def attend_back(nh, dim, rows, tables, slopes, starts, act, pre, d_attended):
    total = act.shape[0]
    blocks = total // rows
    smem = pl.BlockSpec(memory_space=pltpu.SMEM)
    vmem = pl.BlockSpec(memory_space=pltpu.VMEM)
    return pl.pallas_call(
        functools.partial(backward_kernel, nh, dim, rows, blocks),
        out_shape=(
            jax.ShapeDtypeStruct(act.shape, BF),
            jax.ShapeDtypeStruct((nh, 8, rows), F32),
        ),
        in_specs=[smem] * 4 + [vmem] * 4,
        out_specs=(vmem, vmem),
        scratch_shapes=[
            pltpu.VMEM((blocks, rows, rows), F32),
            pltpu.VMEM((rows, nh * dim), F32),
            pltpu.VMEM((total, nh * dim), F32),
            pltpu.VMEM((total, nh * dim), F32),
            pltpu.VMEM((nh, 8, rows), F32),
        ],
        compiler_params=pltpu.CompilerParams(vmem_limit_bytes=48 * 2**20),
        cost_estimate=attention_cost(nh, dim, total, 5),
    )(*tables, slopes, starts, act, pre, d_attended)


def body(
    n_dp, n, tokens, input_norm_gain, proj_in, proj_out, bias_slope, lengths, cotangent
):
    local_rows, width = tokens.shape
    nh, dim = proj_in.shape[1], proj_in.shape[3]
    part = nh * dim
    rows = local_rows // 2
    half = n // 2
    dp = lax.axis_index("dp")
    z = lax.axis_index("head")
    c = dp & 1
    host = (z >= half).astype(jnp.int32)
    is_home = c == host

    def move(x, target):
        pairs = []
        for d in range(n_dp):
            for s in range(n):
                e, t = target(d, s)
                pairs.append((d * n + s, e * n + t))
        return lax.ppermute(x, AXES, pairs)

    def core_swap(x):
        return move(x, lambda d, s: (d ^ 1, s))

    def z_swap(x, bit):
        return move(x, lambda d, s: (d, s ^ bit))

    def dp_swap(x, bit):
        return move(x, lambda d, s: (d ^ bit, s))

    def send_target(r):
        def target(d, s):
            core = int(s >= half)
            return ((d & ~1) | core, s ^ r ^ ((d & 1) * half))

        return target

    def back_target(r):
        forward = {}
        for d in range(n_dp):
            for s in range(n):
                forward[send_target(r)(d, s)] = (d, s)
        return lambda d, s: forward[(d, s)]

    def cross(x):
        return move(x, lambda d, s: (d, s ^ ((d & 1) * half)))

    token_single = tokens.astype(F32)
    centred_input = jnp.mean(token_single, axis=1, keepdims=True)
    spread = jnp.mean((token_single - centred_input) ** 2, axis=1, keepdims=True)
    inverse_deviation = lax.rsqrt(spread + EPSILON)
    xhat = (token_single - centred_input) * inverse_deviation
    normed = (xhat * input_norm_gain).astype(BF)

    first, second = normed[:rows], normed[rows:]
    keep = jnp.where(c == 0, first, second)
    give = jnp.where(c == 0, second, first)
    barrier = lax.optimization_barrier
    bits = [1 << b for b in range(n_dp.bit_length() - 1)]
    slab_o = part // n_dp
    slab_w = 3 * slab_o
    got = core_swap(give)
    w_own, gate_rows = unpack(nh, dim, proj_in, give)
    mirrored = sum(
        jnp.where((dp & b) != 0, bits[-1] // b, 0) for b in bits
    )
    w_slab = lax.dynamic_slice_in_dim(w_own, mirrored * slab_w, slab_w, 0)
    items = {0: jnp.where(is_home, keep, got)}
    crossed = z_swap(jnp.where(is_home, got, keep), half)
    piece = z_swap(w_slab, half)
    bit = 1
    while bit < half:
        for t in sorted(items):
            items[t ^ bit] = z_swap(items[t], bit)
        bit *= 2
    own_lengths = lengths[0]
    hosted_lengths = jnp.where(is_home, own_lengths, core_swap(own_lengths))
    total = n * local_rows
    ends = jnp.cumsum(hosted_lengths)
    positions = jnp.arange(total, dtype=jnp.int32)
    starts = jnp.max(
        jnp.where(positions[:, None] >= ends[None, :], ends[None, :], 0), axis=1, keepdims=True
    ).astype(jnp.int32)
    block = jnp.arange(total // rows, dtype=jnp.int32)
    low = starts[::rows, 0] // rows
    shard = (block // 2) ^ z
    held = ((block & 1) ^ c) * n + shard
    sent = 2 * (shard ^ (c * half)) + (block & 1)
    tables = (low, held, sent)
    slopes = cross(bias_slope)

    items, crossed, piece, tables, starts, slopes = barrier(
        (items, crossed, piece, tables, starts, slopes)
    )

    def dp_double(x, bit, axis):
        other = dp_swap(x, bit)
        up = (dp & bit) != 0
        return jnp.concatenate(
            [jnp.where(up, other, x), jnp.where(up, x, other)], axis=axis
        )

    side = width // 2
    pair = [piece[:, :side], piece[:, side:]]
    pair = [x.reshape([1] * len(bits) + [slab_w, side]) for x in pair]

    def weights_step(pair, k):
        there, here = bits[:0:-1], bits[1:]
        return [
            dp_double(pair[0], there[k], bits.index(there[k])),
            dp_double(pair[1], here[k], bits.index(here[k])),
        ]

    def spread(x):
        found = {half: x}
        bit = 1
        while bit < half:
            for t in sorted(found):
                found[t ^ bit] = z_swap(found[t], bit)
            bit *= 2
        return found

    middle = rows // 2
    upper = spread(crossed[:middle])
    for k in range(len(bits) - 2):
        pair = weights_step(pair, k)
    upper, pair, lower = barrier((upper, pair, crossed[middle:rows]))
    lower = spread(lower)
    pair = weights_step(pair, len(bits) - 2)
    items, upper, lower, pair = barrier((items, upper, lower, pair))
    piece = dp_double(jnp.concatenate(pair, axis=-1), bits[0], 0)
    piece = piece.reshape(3 * part, width)
    for t in upper:
        items[t] = jnp.concatenate([upper[t], lower[t]], axis=0)
    mine = [items[t] for t in range(n)]
    theirs = [core_swap(x) for x in mine]

    slabs = jnp.concatenate(
        [
            lax.dynamic_slice_in_dim(gate_rows, dp * slab_o, slab_o, 0),
            lax.dynamic_slice_in_dim(proj_out.reshape(part, width), dp * slab_o, slab_o, 0),
        ],
        axis=0,
    )
    everything = lax.all_gather(slabs, AXES).reshape(n_dp, n, 2, slab_o, width)

    w_qkv = jnp.where(c == 0, w_own, piece)

    attended, act, pre = attend(
        nh, dim, rows, tables, slopes, starts, w_qkv, mine + theirs
    )
    w_gate, w_out, pre_gate, d_gated = prepare(
        n, n_dp, slab_o, z, everything, normed, cotangent, attended
    )
    mine, theirs, attended = barrier((mine, theirs, attended))
    gathered = jnp.concatenate(mine + theirs, axis=0)
    arrived = [
        move(attended[r * local_rows : (r + 1) * local_rows], send_target(r)) for r in range(n)
    ]
    arrived, w_gate, w_out, pre_gate, d_gated = barrier(
        (arrived, w_gate, w_out, pre_gate, d_gated)
    )
    d_attended, both, gated, d_pre_gate = gate_and_norm(
        n, pre_gate, d_gated, normed, cotangent, arrived
    )

    def add(x, y):
        return (x.astype(F32) + y.astype(F32)).astype(BF)

    order = bits[1:] + bits[:1]
    split = [2] * len(bits)
    forth, back = bits[1:], bits[:0:-1]

    def reduce_bit(x, b, axis):
        up = (dp & b) != 0
        low_half = lax.slice_in_dim(x, 0, 1, axis=axis)
        high_half = lax.slice_in_dim(x, 1, 2, axis=axis)
        return add(
            jnp.where(up, high_half, low_half),
            dp_swap(jnp.where(up, low_half, high_half), b),
        )

    def double_bit(x, b, axis):
        other = dp_swap(x, b)
        up = (dp & b) != 0
        return jnp.concatenate(
            [jnp.where(up, other, x), jnp.where(up, x, other)], axis=axis
        )

    both = both.reshape([2, n] + split + [slab_o, width])
    both = reduce_bit(both, 1, 1 + len(bits))
    arrived = [
        move(d_attended[r], back_target(r)) for r in range(n)
    ]
    d_att = jnp.concatenate(arrived, axis=0)
    pair = [both[0], both[1]]
    def reduce_pair(pair, k, first_axis):
        return [
            reduce_bit(pair[0], forth[k], first_axis + order.index(forth[k])),
            reduce_bit(pair[1], back[k], first_axis + order.index(back[k])),
        ]

    both = reduce_pair(pair, 0, 1)
    mixed = (token_single + dot(gated, w_out)).astype(BF)
    d_normed_gate = dot(d_pre_gate, w_gate)
    d_att, both, mixed, d_normed_gate = barrier((d_att, both, mixed, d_normed_gate))
    for k in range(1, len(forth)):
        both = reduce_pair(both, k, 1)

    d_pre, slope_rows = attend_back(
        nh, dim, rows, tables, slopes, starts, act, pre, d_att
    )

    def partial(first_block, last_block):
        return dot(d_pre[first_block * rows : last_block * rows], w_qkv).astype(BF)

    d_pre, both = barrier((d_pre, both))
    theirs = partial(n, 2 * n)
    got = core_swap(theirs)
    d_pre, theirs = barrier((d_pre, theirs))
    in_part = dot(d_pre, gathered, TN).astype(BF)
    mine = partial(0, n)
    both = jnp.stack(both).reshape(2, n, slab_o, width)
    both = add(both[:, :half], z_swap(both[:, half:], half))
    in_part, got, both = barrier((in_part, got, both))

    side = width // 2
    x = in_part.reshape(split + [slab_w, width])
    pair = reduce_pair([x[..., :side], x[..., side:]], 0, 0)
    home, away = add(mine[: half * rows], got[: half * rows]), add(
        mine[half * rows :], got[half * rows :]
    )
    bit = half // 2
    while bit >= 1:
        away = add(away[: bit * rows], z_swap(away[bit * rows :], bit))
        bit //= 2
    bit = half // 2
    while bit >= 1:
        both = add(both[:, :bit], z_swap(both[:, bit:], bit))
        bit //= 2
    both = both.reshape(2 * slab_o, width)
    for k in range(1, len(forth)):
        pair = reduce_pair(pair, k, 0)
    pair, away, home, both = barrier((pair, away, home, both))

    cuts = [away[k * rows // 4 : (k + 1) * rows // 4] for k in range(4)]
    moved = [z_swap(cuts[0], half)]
    x = cross(jnp.concatenate(pair, axis=-1))
    x, moved, home, both, cuts = barrier((x, moved, home, both, cuts))

    moved.append(z_swap(cuts[1], half))
    x = reduce_bit(x, 1, len(bits) - 1)
    bit = half // 2
    while bit > 1:
        home = add(home[: bit * rows], z_swap(home[bit * rows :], bit))
        bit //= 2
    homes = [home[:middle]]
    if bit:
        homes[0] = add(homes[0], z_swap(home[rows : rows + middle], 1))
    x, moved, cuts, homes, home = barrier((x, moved, cuts, homes, home))
    homes.append(home[middle:rows])
    if bit:
        homes[1] = add(homes[1], z_swap(home[rows + middle :], 1))
    moved.append(z_swap(cuts[2], half))
    x = x.reshape(slab_w, width)
    place = sum(
        jnp.where((dp & b) != 0, 1 << (len(bits) - 1 - i), 0) for i, b in enumerate(order)
    )
    own = jnp.concatenate(
        [
            lax.dynamic_slice_in_dim(w_own, place * slab_w, slab_w, 0),
            lax.dynamic_slice_in_dim(gate_rows, place * slab_o, slab_o, 0),
        ],
        axis=0,
    )
    x = jnp.concatenate([x, both], axis=0)
    gain_part = jnp.sum(x[: slab_w + slab_o].astype(F32) * own.astype(F32), axis=0)
    own_slope = jnp.sum(slope_rows, axis=(1, 2))
    chunk = z ^ (c * half)
    slope_part = jnp.where(jnp.arange(n)[:, None] == chunk, own_slope[None, :], 0.0)
    slope_part = jnp.pad(slope_part.reshape(-1), (0, width - n * nh))
    small = jnp.stack([gain_part, slope_part])
    high = small.astype(BF)
    rest = (small - high.astype(F32)).astype(BF)
    x = jnp.concatenate([x, high, rest, jnp.zeros((12, width), BF)], axis=0)
    x = x.reshape([1] * len(bits) + list(x.shape))

    def double_pair(pair, k):
        return [
            double_bit(pair[0], back[k], order.index(back[k])),
            double_bit(pair[1], forth[k], order.index(forth[k])),
        ]

    pair = double_pair([x[..., :side], x[..., side:]], 0)
    pair, moved, cuts, homes = barrier((pair, moved, cuts, homes))
    home = jnp.concatenate(homes, axis=0)
    moved.append(z_swap(cuts[3], half))
    for k in range(1, len(forth)):
        pair = double_pair(pair, k)
    pair, moved = barrier((pair, moved))
    away = jnp.concatenate(moved, axis=0)
    keep = jnp.where(is_home, home, away)
    got = core_swap(jnp.where(is_home, away, home))
    d_normed = jnp.concatenate(
        [jnp.where(c == 0, keep, got), jnp.where(c == 0, got, keep)], axis=0
    ).astype(F32) + d_normed_gate
    pair = [
        double_bit(y, 1, len(bits) - 1).reshape(n_dp, 5 * slab_o + 16, side) for y in pair
    ]
    grad_proj_in, grad_proj_out = assemble(nh, dim, n_dp, width, *pair)
    grad_proj_in = grad_proj_in.reshape(width, nh, 4, dim)
    grad_proj_out = grad_proj_out.reshape(nh, dim, width)

    small = jnp.concatenate([y[:, 5 * slab_o :] for y in pair], axis=-1).astype(F32)
    small = jnp.sum(small, axis=0)
    small = small[:2] + small[2:4]
    small = small + sum(z_swap(small, t) for t in range(1, n))
    norm_gain_gradient = small[0] / input_norm_gain
    grad_slope = lax.dynamic_slice_in_dim(small[1], z * nh, nh, 0)

    dh = d_normed * input_norm_gain
    token_gradient = cotangent.astype(F32) + inverse_deviation * (
        dh
        - jnp.mean(dh, axis=1, keepdims=True)
        - xhat * jnp.mean(dh * xhat, axis=1, keepdims=True)
    )
    return (mixed, token_gradient, norm_gain_gradient, grad_proj_in, grad_proj_out, grad_slope)


def solution(mesh):
    return jax.shard_map(
        functools.partial(body, mesh.shape["dp"], mesh.shape["head"]),
        mesh=mesh,
        in_specs=(
            P(("dp", "head"), None),
            P(),
            P(None, "head", None, None),
            P("head", None, None),
            P("head"),
            P("dp", None),
            P(("dp", "head"), None),
        ),
        out_specs=(
            P(("dp", "head"), None),
            P(("dp", "head"), None),
            P(),
            P(None, "head", None, None),
            P("head", None, None),
            P("head"),
        ),
        check_vma=False,
    )
```

```python
import functools

import jax
import jax.numpy as jnp
from jax import lax
from jax.experimental import pallas as pl
from jax.experimental.pallas import tpu as pltpu
from jax.sharding import PartitionSpec as P

EPSILON = 1e-05
BF = jnp.bfloat16
F32 = jnp.float32
AXES = ("dp", "head")
NT = (((1,), (1,)), ((), ()))
TN = (((0,), (0,)), ((), ()))
NN = (((1,), (0,)), ((), ()))


def dot(a, b, dims=NN):
    return lax.dot_general(a, b, dims, preferred_element_type=F32)


def silu_slope(values):
    sigma = jax.nn.sigmoid(values)
    return sigma * (1.0 + values * (1.0 - sigma))


def tanh_slope(values):
    sigma = 0.5 + 0.5 * jnp.tanh(0.5 * values)
    return sigma * (1.0 + values * (1.0 - sigma))


def fill_distance(dist, blocks, rows, query_axis):
    row = lax.broadcasted_iota(jnp.int32, (rows, rows), query_axis)
    column = lax.broadcasted_iota(jnp.int32, (rows, rows), 1 - query_axis)

    def one(step, carry):
        offset = jnp.maximum(step * rows + row - column, 0).astype(F32)
        dist[step] = jnp.log(1.0 + offset)
        return carry

    lax.fori_loop(0, blocks, one, 0)


def half_score(q, k, slope, distance, visible, scale):
    u = dot(q, k, NT) * (0.5 * scale) + (0.5 * slope) * distance
    return jnp.where(visible, u, -1.0e4)


def visible_pairs(starts_ref, i, j, rows):
    row = lax.broadcasted_iota(jnp.int32, (rows, rows), 0) + i * rows
    column = lax.broadcasted_iota(jnp.int32, (rows, rows), 1) + j * rows
    first = starts_ref[pl.ds(pl.multiple_of(i * rows, rows), rows), :]
    return (column >= first) & (column <= row)


def forward_kernel(
    nh, dim, rows, blocks, low, held, sent, slopes, starts_ref, w_ref, *refs
):
    pieces = refs[:blocks]
    out_ref, act_hbm, pre_hbm, dist, acc, act_ref, pre_ref, sems = refs[blocks:]
    for b in range(blocks):
        pre = dot(pieces[b][...], w_ref[...], NT)
        half = 0.5 * pre
        pre_ref[b * rows : (b + 1) * rows, :] = pre.astype(BF)
        act_ref[b * rows : (b + 1) * rows, :] = (half + half * jnp.tanh(half)).astype(BF)
    act_copy = pltpu.make_async_copy(act_ref, act_hbm, sems.at[0])
    pre_copy = pltpu.make_async_copy(pre_ref, pre_hbm, sems.at[1])
    act_copy.start()
    pre_copy.start()
    fill_distance(dist, blocks, rows, 0)
    scale = dim ** (-0.5)
    part = nh * dim

    def at(block):
        return pl.ds(pl.multiple_of(block * rows, rows), rows)

    def query_block(i, carry):
        acc[...] = jnp.zeros_like(acc)

        def key_block(j, inner):
            visible = visible_pairs(starts_ref, i, j, rows)
            distance = dist[i - j]
            for h in range(nh):
                q = act_ref[at(held[i]), part + h * dim : part + (h + 1) * dim]
                k = act_ref[at(held[j]), 2 * part + h * dim : 2 * part + (h + 1) * dim]
                v = act_ref[at(held[j]), h * dim : (h + 1) * dim]
                u = half_score(q, k, slopes[h], distance, visible, scale)
                w = (u + u * jnp.tanh(u)).astype(BF)
                acc[:, h * dim : (h + 1) * dim] += dot(w, v)
            return inner

        lax.fori_loop(low[i], i + 1, key_block, 0)
        out_ref[at(sent[i]), :] = acc[...].astype(BF)
        return carry

    lax.fori_loop(0, blocks, query_block, 0)
    act_copy.wait()
    pre_copy.wait()


def backward_kernel(
    nh, dim, rows, blocks, low, held, sent, slopes, starts_ref, act_ref, pre_ref, datt_ref,
    out_ref, slope_ref, dist, dq, dk, dv, gs
):
    fill_distance(dist, blocks, rows, 1)
    scale = dim ** (-0.5)
    part = nh * dim
    dk[...] = jnp.zeros_like(dk)
    dv[...] = jnp.zeros_like(dv)
    gs[...] = jnp.zeros_like(gs)

    def at(block):
        return pl.ds(pl.multiple_of(block * rows, rows), rows)

    def query_block(i, carry):
        dq[...] = jnp.zeros_like(dq)
        mine = held[i]

        def key_block(j, inner):
            key = lax.broadcasted_iota(jnp.int32, (rows, rows), 0) + j * rows
            query = lax.broadcasted_iota(jnp.int32, (rows, rows), 1) + i * rows
            visible = (key >= starts_ref[i]) & (key <= query)
            distance = dist[i - j]
            theirs = held[j]
            for h in range(nh):
                cols = slice(h * dim, (h + 1) * dim)
                q = act_ref[at(mine), part + h * dim : part + (h + 1) * dim]
                k = act_ref[at(theirs), 2 * part + h * dim : 2 * part + (h + 1) * dim]
                v = act_ref[at(theirs), cols]
                da = datt_ref[at(sent[i]), cols]
                u = half_score(k, q, slopes[h], distance, visible, scale)
                t = jnp.tanh(u)
                w = u + u * t
                ds = dot(v, da, NT) * ((1.0 + t) + w * (1.0 - t))
                gs[h] += jnp.sum((ds * distance).reshape(rows // 8, 8, rows), axis=0)
                wb = w.astype(BF)
                db = ds.astype(BF)
                dv[at(theirs), cols] += dot(wb, da)
                dk[at(theirs), cols] += dot(db, q)
                dq[:, cols] += dot(db, k, TN)
            return inner

        lax.fori_loop(low[i], i + 1, key_block, 0)
        slope = tanh_slope(pre_ref[at(mine), part : 2 * part].astype(F32))
        out_ref[at(mine), part : 2 * part] = (dq[...] * (0.5 * scale) * slope).astype(BF)
        return carry

    lax.fori_loop(0, blocks, query_block, 0)

    def finish(b, carry):
        slope_v = tanh_slope(pre_ref[at(b), :part].astype(F32))
        out_ref[at(b), :part] = (dv[at(b), :] * slope_v).astype(BF)
        slope_k = tanh_slope(pre_ref[at(b), 2 * part :].astype(F32))
        out_ref[at(b), 2 * part :] = (dk[at(b), :] * (0.5 * scale) * slope_k).astype(BF)
        return carry

    lax.fori_loop(0, blocks, finish, 0)
    for h in range(nh):
        slope_ref[h] = 0.5 * gs[h]


def attention_cost(nh, dim, total, matmuls):
    pairs = total * total // 5
    return pl.CostEstimate(
        flops=30 * matmuls * nh * dim * pairs,
        bytes_accessed=total * nh * dim * 2 * 2 * matmuls,
        transcendentals=nh * pairs,
    )


def attend(nh, dim, rows, tables, slopes, starts, w, pieces):
    blocks = len(pieces)
    total = blocks * rows
    wide = jax.ShapeDtypeStruct((total, 3 * nh * dim), BF)
    smem = pl.BlockSpec(memory_space=pltpu.SMEM)
    vmem = pl.BlockSpec(memory_space=pltpu.VMEM)
    return pl.pallas_call(
        functools.partial(forward_kernel, nh, dim, rows, blocks),
        out_shape=(jax.ShapeDtypeStruct((total, nh * dim), BF), wide, wide),
        in_specs=[smem] * 4 + [vmem] * (2 + blocks),
        out_specs=(vmem,) + (pl.BlockSpec(memory_space=pltpu.HBM),) * 2,
        scratch_shapes=[
            pltpu.VMEM((blocks, rows, rows), F32),
            pltpu.VMEM((rows, nh * dim), F32),
            pltpu.VMEM(wide.shape, BF),
            pltpu.VMEM(wide.shape, BF),
            pltpu.SemaphoreType.DMA((2,)),
        ],
        compiler_params=pltpu.CompilerParams(vmem_limit_bytes=40 * 2**20),
        cost_estimate=attention_cost(nh, dim, total, 2),
    )(*tables, slopes, starts, w, *pieces)


def unpack_kernel(nh, dim, w_ref, after_ref, own_ref, gate_ref):
    part = nh * dim
    for h in range(nh):
        for kind in range(4):
            x = w_ref[:, h * 4 + kind, :]
            x = x.astype(F32).T.astype(BF)
            at = ((kind - 1) * nh + h) * dim
            if kind:
                own_ref[at : at + dim, :] = x
            else:
                gate_ref[h * dim : (h + 1) * dim, :] = x


def unpack(nh, dim, proj_in, after):
    width = proj_in.shape[0]
    vmem = pl.BlockSpec(memory_space=pltpu.VMEM)
    return pl.pallas_call(
        functools.partial(unpack_kernel, nh, dim),
        out_shape=(
            jax.ShapeDtypeStruct((3 * nh * dim, width), BF),
            jax.ShapeDtypeStruct((nh * dim, width), BF),
        ),
        in_specs=[vmem, pl.BlockSpec(memory_space=pl.ANY)],
        out_specs=(vmem,) * 2,
        compiler_params=pltpu.CompilerParams(vmem_limit_bytes=24 * 2**20),
        cost_estimate=pl.CostEstimate(flops=2 * 10**10, bytes_accessed=8 * 2**20, transcendentals=0),
    )(proj_in.reshape(width, nh * 4, dim), after)


def prepare_kernel(
    n, n_dp, slab, z_ref, all_ref, normed_ref, cot_ref, after_ref,
    gate_w_ref, out_w_ref, pre_gate_ref, d_gated_ref
):
    part = n_dp * slab
    for t in range(n):
        q = z_ref[0] ^ t
        for s in range(n_dp):
            at = t * part + s * slab
            gate_w_ref[at : at + slab, :] = all_ref[s, q, 0]
            out_w_ref[at : at + slab, :] = all_ref[s, q, 1]
    for t in range(n):
        at = slice(t * part, (t + 1) * part)
        pre_gate_ref[:, at] = dot(normed_ref[...], gate_w_ref[at, :], NT)
        d_gated_ref[:, at] = dot(cot_ref[...], out_w_ref[at, :], NT)


def prepare(n, n_dp, slab, z, everything, normed, cotangent, after):
    rows, width = normed.shape
    vmem = pl.BlockSpec(memory_space=pltpu.VMEM)
    columns = n * n_dp * slab
    return pl.pallas_call(
        functools.partial(prepare_kernel, n, n_dp, slab),
        out_shape=(
            jax.ShapeDtypeStruct((columns, width), BF),
            jax.ShapeDtypeStruct((columns, width), BF),
            jax.ShapeDtypeStruct((rows, columns), F32),
            jax.ShapeDtypeStruct((rows, columns), F32),
        ),
        in_specs=[pl.BlockSpec(memory_space=pltpu.SMEM)]
        + [vmem] * 3
        + [pl.BlockSpec(memory_space=pl.ANY)],
        out_specs=(vmem,) * 4,
        compiler_params=pltpu.CompilerParams(vmem_limit_bytes=32 * 2**20),
        cost_estimate=pl.CostEstimate(
            flops=20 * rows * width * columns, bytes_accessed=16 * 2**20, transcendentals=0
        ),
    )(z.reshape(1), everything, normed, cotangent, after)


def gate_kernel(n, step, pre_gate_ref, d_gated_ref, normed_ref, cot_ref, *refs):
    pieces, d_att = refs[:n], refs[n : 2 * n]
    both_ref, gated_ref, d_pre_gate_ref, dn_ref = refs[2 * n :]
    rows, width = pre_gate_ref.shape
    part = width // n

    def some_rows(r, carry):
        at = pl.ds(pl.multiple_of(r * step, step), step)
        att = [ref[at, :].astype(F32) for ref in pieces]
        mean = sum(jnp.sum(x, axis=1, keepdims=True) for x in att) / width
        square = sum(jnp.sum(x * x, axis=1, keepdims=True) for x in att) / width
        inv = lax.rsqrt(square - mean * mean + EPSILON)
        first = jnp.zeros((step, 1), F32)
        second = jnp.zeros((step, 1), F32)
        for t in range(n):
            columns = slice(t * part, (t + 1) * part)
            normed_o = (att[t] - mean) * inv
            pre = pre_gate_ref[at, columns]
            d_gated = d_gated_ref[at, columns]
            sigma = 0.5 + 0.5 * jnp.tanh(0.5 * pre)
            gate = (pre * sigma).astype(BF).astype(F32)
            gated_ref[at, columns] = (normed_o * gate).astype(BF)
            dn = d_gated * gate
            first += jnp.sum(dn, axis=1, keepdims=True)
            second += jnp.sum(dn * normed_o, axis=1, keepdims=True)
            d_gate = (d_gated * normed_o).astype(BF).astype(F32)
            slope = sigma * (1.0 + pre * (1.0 - sigma))
            d_pre_gate_ref[at, columns] = (d_gate * slope).astype(BF)
            dn_ref[:, columns] = dn
        first, second = first / width, second / width
        for t in range(n):
            columns = slice(t * part, (t + 1) * part)
            normed_o = (att[t] - mean) * inv
            dn = dn_ref[:, columns]
            d_att[t][at, :] = (inv * (dn - first - normed_o * second)).astype(BF)
        return carry

    lax.fori_loop(0, rows // step, some_rows, 0)
    for t in range(n):
        columns = slice(t * part, (t + 1) * part)
        both_ref[0, columns, :] = dot(d_pre_gate_ref[:, columns], normed_ref[...], TN).astype(BF)
        both_ref[1, columns, :] = dot(gated_ref[:, columns], cot_ref[...], TN).astype(BF)


def gate_and_norm(n, pre_gate, d_gated, normed, cotangent, pieces):
    rows, width = normed.shape
    columns = pre_gate.shape[1]
    vmem = pl.BlockSpec(memory_space=pltpu.VMEM)
    outs = pl.pallas_call(
        functools.partial(gate_kernel, n, 64),
        out_shape=[jax.ShapeDtypeStruct(x.shape, BF) for x in pieces]
        + [
            jax.ShapeDtypeStruct((2, columns, width), BF),
            jax.ShapeDtypeStruct((rows, columns), BF),
            jax.ShapeDtypeStruct((rows, columns), BF),
        ],
        in_specs=[vmem] * (4 + n),
        out_specs=[vmem] * (n + 3),
        scratch_shapes=[pltpu.VMEM((64, columns), F32)],
        compiler_params=pltpu.CompilerParams(vmem_limit_bytes=32 * 2**20),
        cost_estimate=pl.CostEstimate(
            flops=8 * rows * width * columns, bytes_accessed=16 * 2**20, transcendentals=0
        ),
    )(pre_gate, d_gated, normed, cotangent, *pieces)
    return list(outs[:n]), outs[n], outs[n + 1], outs[n + 2]


def assemble_kernel(nh, dim, n_dp, first_ref, second_ref, in_ref, out_ref, rows_ref):
    part = nh * dim
    slab = part // n_dp
    side = first_ref.shape[2]
    for s in range(n_dp):
        for side_at, ref in ((0, first_ref), (1, second_ref)):
            x = ref[s].astype(F32)
            columns = slice(side_at * side, (side_at + 1) * side)
            rows_ref[3 * s * slab : 3 * (s + 1) * slab, columns] = x[: 3 * slab]
            at = 3 * part + s * slab
            rows_ref[at : at + slab, columns] = x[3 * slab : 4 * slab]
            out_ref[s * slab : (s + 1) * slab, columns] = x[4 * slab : 5 * slab]
    for h in range(nh):
        for kind in range(4):
            at = kind * part + h * dim
            in_ref[:, h * 4 + (kind + 1) % 4, :] = rows_ref[at : at + dim, :].T


def assemble(nh, dim, n_dp, width, first, second):
    vmem = pl.BlockSpec(memory_space=pltpu.VMEM)
    return pl.pallas_call(
        functools.partial(assemble_kernel, nh, dim, n_dp),
        out_shape=(
            jax.ShapeDtypeStruct((width, nh * 4, dim), F32),
            jax.ShapeDtypeStruct((nh * dim, width), F32),
        ),
        in_specs=[vmem] * 2,
        out_specs=(vmem,) * 2,
        scratch_shapes=[pltpu.VMEM((4 * nh * dim, width), F32)],
        compiler_params=pltpu.CompilerParams(vmem_limit_bytes=40 * 2**20),
        cost_estimate=pl.CostEstimate(
            flops=10**10, bytes_accessed=8 * 2**20, transcendentals=0
        ),
    )(first, second)


def attend_back(nh, dim, rows, tables, slopes, starts, act, pre, d_attended):
    total = act.shape[0]
    blocks = total // rows
    smem = pl.BlockSpec(memory_space=pltpu.SMEM)
    vmem = pl.BlockSpec(memory_space=pltpu.VMEM)
    return pl.pallas_call(
        functools.partial(backward_kernel, nh, dim, rows, blocks),
        out_shape=(
            jax.ShapeDtypeStruct(act.shape, BF),
            jax.ShapeDtypeStruct((nh, 8, rows), F32),
        ),
        in_specs=[smem] * 4 + [vmem] * 4,
        out_specs=(vmem, vmem),
        scratch_shapes=[
            pltpu.VMEM((blocks, rows, rows), F32),
            pltpu.VMEM((rows, nh * dim), F32),
            pltpu.VMEM((total, nh * dim), F32),
            pltpu.VMEM((total, nh * dim), F32),
            pltpu.VMEM((nh, 8, rows), F32),
        ],
        compiler_params=pltpu.CompilerParams(vmem_limit_bytes=48 * 2**20),
        cost_estimate=attention_cost(nh, dim, total, 5),
    )(*tables, slopes, starts.reshape(blocks, 1, rows), act, pre, d_attended)


def body(
    n_dp, n, tokens, input_norm_gain, proj_in, proj_out, bias_slope, lengths, cotangent
):
    local_rows, width = tokens.shape
    nh, dim = proj_in.shape[1], proj_in.shape[3]
    part = nh * dim
    rows = local_rows // 2
    half = n // 2
    dp = lax.axis_index("dp")
    z = lax.axis_index("head")
    c = dp & 1
    host = (z >= half).astype(jnp.int32)
    is_home = c == host

    def move(x, target):
        pairs = []
        for d in range(n_dp):
            for s in range(n):
                e, t = target(d, s)
                pairs.append((d * n + s, e * n + t))
        return lax.ppermute(x, AXES, pairs)

    def core_swap(x):
        return move(x, lambda d, s: (d ^ 1, s))

    def z_swap(x, bit):
        return move(x, lambda d, s: (d, s ^ bit))

    def dp_swap(x, bit):
        return move(x, lambda d, s: (d ^ bit, s))

    def send_target(r):
        def target(d, s):
            core = int(s >= half)
            return ((d & ~1) | core, s ^ r ^ ((d & 1) * half))

        return target

    def back_target(r):
        forward = {}
        for d in range(n_dp):
            for s in range(n):
                forward[send_target(r)(d, s)] = (d, s)
        return lambda d, s: forward[(d, s)]

    def cross(x):
        return move(x, lambda d, s: (d, s ^ ((d & 1) * half)))

    token_single = tokens.astype(F32)
    centred_input = jnp.mean(token_single, axis=1, keepdims=True)
    spread = jnp.mean((token_single - centred_input) ** 2, axis=1, keepdims=True)
    inverse_deviation = lax.rsqrt(spread + EPSILON)
    xhat = (token_single - centred_input) * inverse_deviation
    normed = (xhat * input_norm_gain).astype(BF)

    first, second = normed[:rows], normed[rows:]
    keep = jnp.where(c == 0, first, second)
    give = jnp.where(c == 0, second, first)
    barrier = lax.optimization_barrier
    bits = [1 << b for b in range(n_dp.bit_length() - 1)]
    slab_o = part // n_dp
    slab_w = 3 * slab_o
    got = core_swap(give)
    w_own, gate_rows = unpack(nh, dim, proj_in, give)
    mirrored = sum(
        jnp.where((dp & b) != 0, bits[-1] // b, 0) for b in bits
    )
    w_slab = lax.dynamic_slice_in_dim(w_own, mirrored * slab_w, slab_w, 0)
    items = {0: jnp.where(is_home, keep, got)}
    crossed = z_swap(jnp.where(is_home, got, keep), half)
    piece = z_swap(w_slab, half)
    bit = 1
    while bit < half:
        for t in sorted(items):
            items[t ^ bit] = z_swap(items[t], bit)
        bit *= 2
    own_lengths = lengths[0]
    hosted_lengths = jnp.where(is_home, own_lengths, core_swap(own_lengths))
    total = n * local_rows
    ends = jnp.cumsum(hosted_lengths)
    positions = jnp.arange(total, dtype=jnp.int32)
    starts = jnp.max(
        jnp.where(positions[:, None] >= ends[None, :], ends[None, :], 0), axis=1, keepdims=True
    ).astype(jnp.int32)
    block = jnp.arange(total // rows, dtype=jnp.int32)
    low = starts[::rows, 0] // rows
    shard = (block // 2) ^ z
    held = ((block & 1) ^ c) * n + shard
    sent = 2 * (shard ^ (c * half)) + (block & 1)
    tables = (low, held, sent)
    slopes = cross(bias_slope)

    items, crossed, piece, tables, starts, slopes = barrier(
        (items, crossed, piece, tables, starts, slopes)
    )

    def dp_double(x, bit, axis):
        other = dp_swap(x, bit)
        up = (dp & bit) != 0
        return jnp.concatenate(
            [jnp.where(up, other, x), jnp.where(up, x, other)], axis=axis
        )

    side = width // 2
    pair = [piece[:, :side], piece[:, side:]]
    pair = [x.reshape([1] * len(bits) + [slab_w, side]) for x in pair]

    def weights_step(pair, k):
        there, here = bits[:0:-1], bits[1:]
        return [
            dp_double(pair[0], there[k], bits.index(there[k])),
            dp_double(pair[1], here[k], bits.index(here[k])),
        ]

    def spread(x):
        found = {half: x}
        bit = 1
        while bit < half:
            for t in sorted(found):
                found[t ^ bit] = z_swap(found[t], bit)
            bit *= 2
        return found

    middle = rows // 2
    upper = spread(crossed[:middle])
    for k in range(len(bits) - 2):
        pair = weights_step(pair, k)
    upper, pair, lower = barrier((upper, pair, crossed[middle:rows]))
    lower = spread(lower)
    pair = weights_step(pair, len(bits) - 2)
    items, upper, lower, pair = barrier((items, upper, lower, pair))
    piece = dp_double(jnp.concatenate(pair, axis=-1), bits[0], 0)
    piece = piece.reshape(3 * part, width)
    for t in upper:
        items[t] = jnp.concatenate([upper[t], lower[t]], axis=0)
    mine = [items[t] for t in range(n)]
    theirs = [core_swap(x) for x in mine]

    slabs = jnp.concatenate(
        [
            lax.dynamic_slice_in_dim(gate_rows, dp * slab_o, slab_o, 0),
            lax.dynamic_slice_in_dim(proj_out.reshape(part, width), dp * slab_o, slab_o, 0),
        ],
        axis=0,
    )
    everything = lax.all_gather(slabs, AXES).reshape(n_dp, n, 2, slab_o, width)

    w_qkv = jnp.where(c == 0, w_own, piece)

    attended, act, pre = attend(
        nh, dim, rows, tables, slopes, starts, w_qkv, mine + theirs
    )
    w_gate, w_out, pre_gate, d_gated = prepare(
        n, n_dp, slab_o, z, everything, normed, cotangent, attended
    )
    mine, theirs, attended = barrier((mine, theirs, attended))
    gathered = jnp.concatenate(mine + theirs, axis=0)
    arrived = [
        move(attended[r * local_rows : (r + 1) * local_rows], send_target(r)) for r in range(n)
    ]
    arrived, w_gate, w_out, pre_gate, d_gated = barrier(
        (arrived, w_gate, w_out, pre_gate, d_gated)
    )
    d_attended, both, gated, d_pre_gate = gate_and_norm(
        n, pre_gate, d_gated, normed, cotangent, arrived
    )

    def add(x, y):
        return (x.astype(F32) + y.astype(F32)).astype(BF)

    order = bits[1:] + bits[:1]
    split = [2] * len(bits)
    forth, back = bits[1:], bits[:0:-1]

    def reduce_bit(x, b, axis):
        up = (dp & b) != 0
        low_half = lax.slice_in_dim(x, 0, 1, axis=axis)
        high_half = lax.slice_in_dim(x, 1, 2, axis=axis)
        return add(
            jnp.where(up, high_half, low_half),
            dp_swap(jnp.where(up, low_half, high_half), b),
        )

    def double_bit(x, b, axis):
        other = dp_swap(x, b)
        up = (dp & b) != 0
        return jnp.concatenate(
            [jnp.where(up, other, x), jnp.where(up, x, other)], axis=axis
        )

    both = both.reshape([2, n] + split + [slab_o, width])
    both = reduce_bit(both, 1, 1 + len(bits))
    arrived = [
        move(d_attended[r], back_target(r)) for r in range(n)
    ]
    d_att = jnp.concatenate(arrived, axis=0)
    pair = [both[0], both[1]]
    def reduce_pair(pair, k, first_axis):
        return [
            reduce_bit(pair[0], forth[k], first_axis + order.index(forth[k])),
            reduce_bit(pair[1], back[k], first_axis + order.index(back[k])),
        ]

    both = reduce_pair(pair, 0, 1)
    mixed = (token_single + dot(gated, w_out)).astype(BF)
    d_normed_gate = dot(d_pre_gate, w_gate)
    d_att, both, mixed, d_normed_gate = barrier((d_att, both, mixed, d_normed_gate))
    for k in range(1, len(forth)):
        both = reduce_pair(both, k, 1)

    d_pre, slope_rows = attend_back(
        nh, dim, rows, tables, slopes, starts, act, pre, d_att
    )

    def partial(first_block, last_block):
        return dot(d_pre[first_block * rows : last_block * rows], w_qkv).astype(BF)

    d_pre, both = barrier((d_pre, both))
    theirs = partial(n, 2 * n)
    got = core_swap(theirs)
    d_pre, theirs = barrier((d_pre, theirs))
    in_part = dot(d_pre, gathered, TN).astype(BF)
    mine = partial(0, n)
    both = jnp.stack(both).reshape(2, n, slab_o, width)
    both = add(both[:, :half], z_swap(both[:, half:], half))
    in_part, got, both = barrier((in_part, got, both))

    side = width // 2
    x = in_part.reshape(split + [slab_w, width])
    pair = reduce_pair([x[..., :side], x[..., side:]], 0, 0)
    home, away = add(mine[: half * rows], got[: half * rows]), add(
        mine[half * rows :], got[half * rows :]
    )
    bit = half // 2
    while bit >= 1:
        away = add(away[: bit * rows], z_swap(away[bit * rows :], bit))
        bit //= 2
    bit = half // 2
    while bit >= 1:
        both = add(both[:, :bit], z_swap(both[:, bit:], bit))
        bit //= 2
    both = both.reshape(2 * slab_o, width)
    for k in range(1, len(forth)):
        pair = reduce_pair(pair, k, 0)
    pair, away, home, both = barrier((pair, away, home, both))

    cuts = [away[k * rows // 4 : (k + 1) * rows // 4] for k in range(4)]
    moved = [z_swap(cuts[0], half)]
    x = cross(jnp.concatenate(pair, axis=-1))
    x, moved, home, both, cuts = barrier((x, moved, home, both, cuts))

    moved.append(z_swap(cuts[1], half))
    x = reduce_bit(x, 1, len(bits) - 1)
    bit = half // 2
    while bit > 1:
        home = add(home[: bit * rows], z_swap(home[bit * rows :], bit))
        bit //= 2
    homes = [home[:middle]]
    if bit:
        homes[0] = add(homes[0], z_swap(home[rows : rows + middle], 1))
    x, moved, cuts, homes, home = barrier((x, moved, cuts, homes, home))
    homes.append(home[middle:rows])
    if bit:
        homes[1] = add(homes[1], z_swap(home[rows + middle :], 1))
    moved.append(z_swap(cuts[2], half))
    x = x.reshape(slab_w, width)
    place = sum(
        jnp.where((dp & b) != 0, 1 << (len(bits) - 1 - i), 0) for i, b in enumerate(order)
    )
    own = jnp.concatenate(
        [
            lax.dynamic_slice_in_dim(w_own, place * slab_w, slab_w, 0),
            lax.dynamic_slice_in_dim(gate_rows, place * slab_o, slab_o, 0),
        ],
        axis=0,
    )
    x = jnp.concatenate([x, both], axis=0)
    gain_part = jnp.sum(x[: slab_w + slab_o].astype(F32) * own.astype(F32), axis=0)
    own_slope = jnp.sum(slope_rows, axis=(1, 2))
    chunk = z ^ (c * half)
    slope_part = jnp.where(jnp.arange(n)[:, None] == chunk, own_slope[None, :], 0.0)
    slope_part = jnp.pad(slope_part.reshape(-1), (0, width - n * nh))
    small = jnp.stack([gain_part, slope_part])
    high = small.astype(BF)
    rest = (small - high.astype(F32)).astype(BF)
    x = jnp.concatenate([x, high, rest, jnp.zeros((12, width), BF)], axis=0)
    x = x.reshape([1] * len(bits) + list(x.shape))

    def double_pair(pair, k):
        return [
            double_bit(pair[0], back[k], order.index(back[k])),
            double_bit(pair[1], forth[k], order.index(forth[k])),
        ]

    pair = double_pair([x[..., :side], x[..., side:]], 0)
    pair, moved, cuts, homes = barrier((pair, moved, cuts, homes))
    home = jnp.concatenate(homes, axis=0)
    moved.append(z_swap(cuts[3], half))
    for k in range(1, len(forth)):
        pair = double_pair(pair, k)
    pair, moved = barrier((pair, moved))
    away = jnp.concatenate(moved, axis=0)
    keep = jnp.where(is_home, home, away)
    got = core_swap(jnp.where(is_home, away, home))
    d_normed = jnp.concatenate(
        [jnp.where(c == 0, keep, got), jnp.where(c == 0, got, keep)], axis=0
    ).astype(F32) + d_normed_gate
    pair = [
        double_bit(y, 1, len(bits) - 1).reshape(n_dp, 5 * slab_o + 16, side) for y in pair
    ]
    grad_proj_in, grad_proj_out = assemble(nh, dim, n_dp, width, *pair)
    grad_proj_in = grad_proj_in.reshape(width, nh, 4, dim)
    grad_proj_out = grad_proj_out.reshape(nh, dim, width)

    small = jnp.concatenate([y[:, 5 * slab_o :] for y in pair], axis=-1).astype(F32)
    small = jnp.sum(small, axis=0)
    small = small[:2] + small[2:4]
    small = small + sum(z_swap(small, t) for t in range(1, n))
    norm_gain_gradient = small[0] / input_norm_gain
    grad_slope = lax.dynamic_slice_in_dim(small[1], z * nh, nh, 0)

    dh = d_normed * input_norm_gain
    token_gradient = cotangent.astype(F32) + inverse_deviation * (
        dh
        - jnp.mean(dh, axis=1, keepdims=True)
        - xhat * jnp.mean(dh * xhat, axis=1, keepdims=True)
    )
    return (mixed, token_gradient, norm_gain_gradient, grad_proj_in, grad_proj_out, grad_slope)


def solution(mesh):
    return jax.shard_map(
        functools.partial(body, mesh.shape["dp"], mesh.shape["head"]),
        mesh=mesh,
        in_specs=(
            P(("dp", "head"), None),
            P(),
            P(None, "head", None, None),
            P("head", None, None),
            P("head"),
            P("dp", None),
            P(("dp", "head"), None),
        ),
        out_specs=(
            P(("dp", "head"), None),
            P(("dp", "head"), None),
            P(),
            P(None, "head", None, None),
            P("head", None, None),
            P("head"),
        ),
        check_vma=False,
    )
```

```python
import functools

import jax
import jax.numpy as jnp
from jax import lax
from jax.experimental import pallas as pl
from jax.experimental.pallas import tpu as pltpu
from jax.sharding import PartitionSpec as P

EPSILON = 1e-05
BF = jnp.bfloat16
F32 = jnp.float32
AXES = ("dp", "head")
NT = (((1,), (1,)), ((), ()))
TN = (((0,), (0,)), ((), ()))
NN = (((1,), (0,)), ((), ()))


def dot(a, b, dims=NN):
    return lax.dot_general(a, b, dims, preferred_element_type=F32)


def silu_slope(values):
    sigma = jax.nn.sigmoid(values)
    return sigma * (1.0 + values * (1.0 - sigma))


def tanh_slope(values):
    sigma = 0.5 + 0.5 * jnp.tanh(0.5 * values)
    return sigma * (1.0 + values * (1.0 - sigma))


def fill_distance(dist, blocks, rows, query_axis):
    row = lax.broadcasted_iota(jnp.int32, (rows, rows), query_axis)
    column = lax.broadcasted_iota(jnp.int32, (rows, rows), 1 - query_axis)

    def one(step, carry):
        offset = jnp.maximum(step * rows + row - column, 0).astype(F32)
        dist[step] = jnp.log(1.0 + offset)
        return carry

    lax.fori_loop(0, blocks, one, 0)


def half_score(q, k, slope, distance, visible, scale):
    u = dot(q, k, NT) * (0.5 * scale) + (0.5 * slope) * distance
    return jnp.where(visible, u, -1.0e4)


def visible_pairs(starts_ref, i, j, rows):
    row = lax.broadcasted_iota(jnp.int32, (rows, rows), 0) + i * rows
    column = lax.broadcasted_iota(jnp.int32, (rows, rows), 1) + j * rows
    first = starts_ref[pl.ds(pl.multiple_of(i * rows, rows), rows), :]
    return (column >= first) & (column <= row)


def forward_kernel(
    nh, dim, rows, blocks, low, held, sent, slopes, starts_ref, w_ref, *refs
):
    pieces = refs[:blocks]
    outs = refs[blocks : blocks + blocks // 2]
    act_hbm, pre_hbm, dist, acc, act_ref, pre_ref, sems, out_ref = refs[blocks + blocks // 2 :]
    for b in range(blocks):
        pre = dot(pieces[b][...], w_ref[...], NT)
        half = 0.5 * pre
        pre_ref[b * rows : (b + 1) * rows, :] = pre.astype(BF)
        act_ref[b * rows : (b + 1) * rows, :] = (half + half * jnp.tanh(half)).astype(BF)
    act_copy = pltpu.make_async_copy(act_ref, act_hbm, sems.at[0])
    pre_copy = pltpu.make_async_copy(pre_ref, pre_hbm, sems.at[1])
    act_copy.start()
    pre_copy.start()
    fill_distance(dist, blocks, rows, 0)
    scale = dim ** (-0.5)
    part = nh * dim

    def at(block):
        return pl.ds(pl.multiple_of(block * rows, rows), rows)

    def query_block(i, carry):
        acc[...] = jnp.zeros_like(acc)

        def key_block(j, inner):
            visible = visible_pairs(starts_ref, i, j, rows)
            distance = dist[i - j]
            for h in range(nh):
                q = act_ref[at(held[i]), part + h * dim : part + (h + 1) * dim]
                k = act_ref[at(held[j]), 2 * part + h * dim : 2 * part + (h + 1) * dim]
                v = act_ref[at(held[j]), h * dim : (h + 1) * dim]
                u = half_score(q, k, slopes[h], distance, visible, scale)
                w = (u + u * jnp.tanh(u)).astype(BF)
                acc[:, h * dim : (h + 1) * dim] += dot(w, v)
            return inner

        lax.fori_loop(low[i], i + 1, key_block, 0)
        out_ref[at(sent[i]), :] = acc[...].astype(BF)
        return carry

    lax.fori_loop(0, blocks, query_block, 0)
    for r, ref in enumerate(outs):
        ref[...] = out_ref[2 * r * rows : 2 * (r + 1) * rows, :]
    act_copy.wait()
    pre_copy.wait()


def backward_kernel(
    nh, dim, rows, blocks, low, held, sent, slopes, starts_ref, act_ref, pre_ref, datt_ref,
    out_ref, slope_ref, dist, dq, dk, dv, gs
):
    fill_distance(dist, blocks, rows, 1)
    scale = dim ** (-0.5)
    part = nh * dim
    dk[...] = jnp.zeros_like(dk)
    dv[...] = jnp.zeros_like(dv)
    gs[...] = jnp.zeros_like(gs)

    def at(block):
        return pl.ds(pl.multiple_of(block * rows, rows), rows)

    def query_block(i, carry):
        dq[...] = jnp.zeros_like(dq)
        mine = held[i]

        def key_block(j, inner):
            key = lax.broadcasted_iota(jnp.int32, (rows, rows), 0) + j * rows
            query = lax.broadcasted_iota(jnp.int32, (rows, rows), 1) + i * rows
            visible = (key >= starts_ref[i]) & (key <= query)
            distance = dist[i - j]
            theirs = held[j]
            for h in range(nh):
                cols = slice(h * dim, (h + 1) * dim)
                q = act_ref[at(mine), part + h * dim : part + (h + 1) * dim]
                k = act_ref[at(theirs), 2 * part + h * dim : 2 * part + (h + 1) * dim]
                v = act_ref[at(theirs), cols]
                da = datt_ref[at(sent[i]), cols]
                u = half_score(k, q, slopes[h], distance, visible, scale)
                t = jnp.tanh(u)
                w = u + u * t
                ds = dot(v, da, NT) * ((1.0 + t) + w * (1.0 - t))
                gs[h] += jnp.sum((ds * distance).reshape(rows // 8, 8, rows), axis=0)
                wb = w.astype(BF)
                db = ds.astype(BF)
                dv[at(theirs), cols] += dot(wb, da)
                dk[at(theirs), cols] += dot(db, q)
                dq[:, cols] += dot(db, k, TN)
            return inner

        lax.fori_loop(low[i], i + 1, key_block, 0)
        slope = tanh_slope(pre_ref[at(mine), part : 2 * part].astype(F32))
        out_ref[at(mine), part : 2 * part] = (dq[...] * (0.5 * scale) * slope).astype(BF)
        return carry

    lax.fori_loop(0, blocks, query_block, 0)

    def finish(b, carry):
        slope_v = tanh_slope(pre_ref[at(b), :part].astype(F32))
        out_ref[at(b), :part] = (dv[at(b), :] * slope_v).astype(BF)
        slope_k = tanh_slope(pre_ref[at(b), 2 * part :].astype(F32))
        out_ref[at(b), 2 * part :] = (dk[at(b), :] * (0.5 * scale) * slope_k).astype(BF)
        return carry

    lax.fori_loop(0, blocks, finish, 0)
    for h in range(nh):
        slope_ref[h] = 0.5 * gs[h]


def attention_cost(nh, dim, total, matmuls):
    pairs = total * total // 5
    return pl.CostEstimate(
        flops=30 * matmuls * nh * dim * pairs,
        bytes_accessed=total * nh * dim * 2 * 2 * matmuls,
        transcendentals=nh * pairs,
    )


def attend(nh, dim, rows, tables, slopes, starts, w, pieces):
    blocks = len(pieces)
    total = blocks * rows
    wide = jax.ShapeDtypeStruct((total, 3 * nh * dim), BF)
    smem = pl.BlockSpec(memory_space=pltpu.SMEM)
    vmem = pl.BlockSpec(memory_space=pltpu.VMEM)
    return pl.pallas_call(
        functools.partial(forward_kernel, nh, dim, rows, blocks),
        out_shape=(jax.ShapeDtypeStruct((2 * rows, nh * dim), BF),) * (blocks // 2)
        + (wide, wide),
        in_specs=[smem] * 4 + [vmem] * (2 + blocks),
        out_specs=(vmem,) * (blocks // 2) + (pl.BlockSpec(memory_space=pltpu.HBM),) * 2,
        scratch_shapes=[
            pltpu.VMEM((blocks, rows, rows), F32),
            pltpu.VMEM((rows, nh * dim), F32),
            pltpu.VMEM(wide.shape, BF),
            pltpu.VMEM(wide.shape, BF),
            pltpu.SemaphoreType.DMA((2,)),
            pltpu.VMEM((total, nh * dim), BF),
        ],
        compiler_params=pltpu.CompilerParams(vmem_limit_bytes=40 * 2**20),
        cost_estimate=attention_cost(nh, dim, total, 2),
    )(*tables, slopes, starts, w, *pieces)


def unpack_kernel(nh, dim, w_ref, after_ref, own_ref, gate_ref):
    part = nh * dim
    for h in range(nh):
        for kind in range(4):
            x = w_ref[:, h * 4 + kind, :]
            x = x.astype(F32).T.astype(BF)
            at = ((kind - 1) * nh + h) * dim
            if kind:
                own_ref[at : at + dim, :] = x
            else:
                gate_ref[h * dim : (h + 1) * dim, :] = x


def unpack(nh, dim, proj_in, after):
    width = proj_in.shape[0]
    vmem = pl.BlockSpec(memory_space=pltpu.VMEM)
    return pl.pallas_call(
        functools.partial(unpack_kernel, nh, dim),
        out_shape=(
            jax.ShapeDtypeStruct((3 * nh * dim, width), BF),
            jax.ShapeDtypeStruct((nh * dim, width), BF),
        ),
        in_specs=[vmem, pl.BlockSpec(memory_space=pl.ANY)],
        out_specs=(vmem,) * 2,
        compiler_params=pltpu.CompilerParams(vmem_limit_bytes=24 * 2**20),
        cost_estimate=pl.CostEstimate(flops=2 * 10**10, bytes_accessed=8 * 2**20, transcendentals=0),
    )(proj_in.reshape(width, nh * 4, dim), after)


def prepare_kernel(
    n, n_dp, slab, z_ref, all_ref, normed_ref, cot_ref, after_ref,
    gate_w_ref, out_w_ref, pre_gate_ref, d_gated_ref
):
    part = n_dp * slab
    for t in range(n):
        q = z_ref[0] ^ t
        for s in range(n_dp):
            at = t * part + s * slab
            gate_w_ref[at : at + slab, :] = all_ref[s, q, 0]
            out_w_ref[at : at + slab, :] = all_ref[s, q, 1]
    for t in range(n):
        at = slice(t * part, (t + 1) * part)
        pre_gate_ref[:, at] = dot(normed_ref[...], gate_w_ref[at, :], NT)
        d_gated_ref[:, at] = dot(cot_ref[...], out_w_ref[at, :], NT)


def prepare(n, n_dp, slab, z, everything, normed, cotangent, after):
    rows, width = normed.shape
    vmem = pl.BlockSpec(memory_space=pltpu.VMEM)
    columns = n * n_dp * slab
    return pl.pallas_call(
        functools.partial(prepare_kernel, n, n_dp, slab),
        out_shape=(
            jax.ShapeDtypeStruct((columns, width), BF),
            jax.ShapeDtypeStruct((columns, width), BF),
            jax.ShapeDtypeStruct((rows, columns), F32),
            jax.ShapeDtypeStruct((rows, columns), F32),
        ),
        in_specs=[pl.BlockSpec(memory_space=pltpu.SMEM)]
        + [vmem] * 3
        + [pl.BlockSpec(memory_space=pl.ANY)],
        out_specs=(vmem,) * 4,
        compiler_params=pltpu.CompilerParams(vmem_limit_bytes=32 * 2**20),
        cost_estimate=pl.CostEstimate(
            flops=20 * rows * width * columns, bytes_accessed=16 * 2**20, transcendentals=0
        ),
    )(z.reshape(1), everything, normed, cotangent, after)


def gate_kernel(n, step, pre_gate_ref, d_gated_ref, normed_ref, cot_ref, *refs):
    pieces, d_att = refs[:n], refs[n : 2 * n]
    both_ref, gated_ref, d_pre_gate_ref, dn_ref = refs[2 * n :]
    rows, width = pre_gate_ref.shape
    part = width // n

    def some_rows(r, carry):
        at = pl.ds(pl.multiple_of(r * step, step), step)
        att = [ref[at, :].astype(F32) for ref in pieces]
        mean = sum(jnp.sum(x, axis=1, keepdims=True) for x in att) / width
        square = sum(jnp.sum(x * x, axis=1, keepdims=True) for x in att) / width
        inv = lax.rsqrt(square - mean * mean + EPSILON)
        first = jnp.zeros((step, 1), F32)
        second = jnp.zeros((step, 1), F32)
        for t in range(n):
            columns = slice(t * part, (t + 1) * part)
            normed_o = (att[t] - mean) * inv
            pre = pre_gate_ref[at, columns]
            d_gated = d_gated_ref[at, columns]
            sigma = 0.5 + 0.5 * jnp.tanh(0.5 * pre)
            gate = (pre * sigma).astype(BF).astype(F32)
            gated_ref[at, columns] = (normed_o * gate).astype(BF)
            dn = d_gated * gate
            first += jnp.sum(dn, axis=1, keepdims=True)
            second += jnp.sum(dn * normed_o, axis=1, keepdims=True)
            d_gate = (d_gated * normed_o).astype(BF).astype(F32)
            slope = sigma * (1.0 + pre * (1.0 - sigma))
            d_pre_gate_ref[at, columns] = (d_gate * slope).astype(BF)
            dn_ref[:, columns] = dn
        first, second = first / width, second / width
        for t in range(n):
            columns = slice(t * part, (t + 1) * part)
            normed_o = (att[t] - mean) * inv
            dn = dn_ref[:, columns]
            d_att[t][at, :] = (inv * (dn - first - normed_o * second)).astype(BF)
        return carry

    lax.fori_loop(0, rows // step, some_rows, 0)
    for t in range(n):
        columns = slice(t * part, (t + 1) * part)
        both_ref[0, columns, :] = dot(d_pre_gate_ref[:, columns], normed_ref[...], TN).astype(BF)
        both_ref[1, columns, :] = dot(gated_ref[:, columns], cot_ref[...], TN).astype(BF)


def gate_and_norm(n, pre_gate, d_gated, normed, cotangent, pieces):
    rows, width = normed.shape
    columns = pre_gate.shape[1]
    vmem = pl.BlockSpec(memory_space=pltpu.VMEM)
    outs = pl.pallas_call(
        functools.partial(gate_kernel, n, 64),
        out_shape=[jax.ShapeDtypeStruct(x.shape, BF) for x in pieces]
        + [
            jax.ShapeDtypeStruct((2, columns, width), BF),
            jax.ShapeDtypeStruct((rows, columns), BF),
            jax.ShapeDtypeStruct((rows, columns), BF),
        ],
        in_specs=[vmem] * (4 + n),
        out_specs=[vmem] * (n + 3),
        scratch_shapes=[pltpu.VMEM((64, columns), F32)],
        compiler_params=pltpu.CompilerParams(vmem_limit_bytes=32 * 2**20),
        cost_estimate=pl.CostEstimate(
            flops=8 * rows * width * columns, bytes_accessed=16 * 2**20, transcendentals=0
        ),
    )(pre_gate, d_gated, normed, cotangent, *pieces)
    return list(outs[:n]), outs[n], outs[n + 1], outs[n + 2]


def assemble_kernel(nh, dim, n_dp, first_ref, second_ref, in_ref, out_ref, rows_ref):
    part = nh * dim
    slab = part // n_dp
    side = first_ref.shape[2]
    for s in range(n_dp):
        for side_at, ref in ((0, first_ref), (1, second_ref)):
            x = ref[s].astype(F32)
            columns = slice(side_at * side, (side_at + 1) * side)
            rows_ref[3 * s * slab : 3 * (s + 1) * slab, columns] = x[: 3 * slab]
            at = 3 * part + s * slab
            rows_ref[at : at + slab, columns] = x[3 * slab : 4 * slab]
            out_ref[s * slab : (s + 1) * slab, columns] = x[4 * slab : 5 * slab]
    for h in range(nh):
        for kind in range(4):
            at = kind * part + h * dim
            in_ref[:, h * 4 + (kind + 1) % 4, :] = rows_ref[at : at + dim, :].T


def assemble(nh, dim, n_dp, width, first, second):
    vmem = pl.BlockSpec(memory_space=pltpu.VMEM)
    return pl.pallas_call(
        functools.partial(assemble_kernel, nh, dim, n_dp),
        out_shape=(
            jax.ShapeDtypeStruct((width, nh * 4, dim), F32),
            jax.ShapeDtypeStruct((nh * dim, width), F32),
        ),
        in_specs=[vmem] * 2,
        out_specs=(vmem,) * 2,
        scratch_shapes=[pltpu.VMEM((4 * nh * dim, width), F32)],
        compiler_params=pltpu.CompilerParams(vmem_limit_bytes=40 * 2**20),
        cost_estimate=pl.CostEstimate(
            flops=10**10, bytes_accessed=8 * 2**20, transcendentals=0
        ),
    )(first, second)


def attend_back(nh, dim, rows, tables, slopes, starts, act, pre, d_attended):
    total = act.shape[0]
    blocks = total // rows
    smem = pl.BlockSpec(memory_space=pltpu.SMEM)
    vmem = pl.BlockSpec(memory_space=pltpu.VMEM)
    return pl.pallas_call(
        functools.partial(backward_kernel, nh, dim, rows, blocks),
        out_shape=(
            jax.ShapeDtypeStruct(act.shape, BF),
            jax.ShapeDtypeStruct((nh, 8, rows), F32),
        ),
        in_specs=[smem] * 4 + [vmem] * 4,
        out_specs=(vmem, vmem),
        scratch_shapes=[
            pltpu.VMEM((blocks, rows, rows), F32),
            pltpu.VMEM((rows, nh * dim), F32),
            pltpu.VMEM((total, nh * dim), F32),
            pltpu.VMEM((total, nh * dim), F32),
            pltpu.VMEM((nh, 8, rows), F32),
        ],
        compiler_params=pltpu.CompilerParams(vmem_limit_bytes=48 * 2**20),
        cost_estimate=attention_cost(nh, dim, total, 5),
    )(*tables, slopes, starts.reshape(blocks, 1, rows), act, pre, d_attended)


def body(
    n_dp, n, tokens, input_norm_gain, proj_in, proj_out, bias_slope, lengths, cotangent
):
    local_rows, width = tokens.shape
    nh, dim = proj_in.shape[1], proj_in.shape[3]
    part = nh * dim
    rows = local_rows // 2
    half = n // 2
    dp = lax.axis_index("dp")
    z = lax.axis_index("head")
    c = dp & 1
    host = (z >= half).astype(jnp.int32)
    is_home = c == host

    def move(x, target):
        pairs = []
        for d in range(n_dp):
            for s in range(n):
                e, t = target(d, s)
                pairs.append((d * n + s, e * n + t))
        return lax.ppermute(x, AXES, pairs)

    def core_swap(x):
        return move(x, lambda d, s: (d ^ 1, s))

    def z_swap(x, bit):
        return move(x, lambda d, s: (d, s ^ bit))

    def dp_swap(x, bit):
        return move(x, lambda d, s: (d ^ bit, s))

    def send_target(r):
        def target(d, s):
            core = int(s >= half)
            return ((d & ~1) | core, s ^ r ^ ((d & 1) * half))

        return target

    def back_target(r):
        forward = {}
        for d in range(n_dp):
            for s in range(n):
                forward[send_target(r)(d, s)] = (d, s)
        return lambda d, s: forward[(d, s)]

    def cross(x):
        return move(x, lambda d, s: (d, s ^ ((d & 1) * half)))

    token_single = tokens.astype(F32)
    centred_input = jnp.mean(token_single, axis=1, keepdims=True)
    spread = jnp.mean((token_single - centred_input) ** 2, axis=1, keepdims=True)
    inverse_deviation = lax.rsqrt(spread + EPSILON)
    xhat = (token_single - centred_input) * inverse_deviation
    normed = (xhat * input_norm_gain).astype(BF)

    first, second = normed[:rows], normed[rows:]
    keep = jnp.where(c == 0, first, second)
    give = jnp.where(c == 0, second, first)
    barrier = lax.optimization_barrier
    bits = [1 << b for b in range(n_dp.bit_length() - 1)]
    slab_o = part // n_dp
    slab_w = 3 * slab_o
    got = core_swap(give)
    w_own, gate_rows = unpack(nh, dim, proj_in, give)
    mirrored = sum(
        jnp.where((dp & b) != 0, bits[-1] // b, 0) for b in bits
    )
    w_slab = lax.dynamic_slice_in_dim(w_own, mirrored * slab_w, slab_w, 0)
    items = {0: jnp.where(is_home, keep, got)}
    crossed = z_swap(jnp.where(is_home, got, keep), half)
    piece = z_swap(w_slab, half)
    bit = 1
    while bit < half:
        for t in sorted(items):
            items[t ^ bit] = z_swap(items[t], bit)
        bit *= 2
    own_lengths = lengths[0]
    hosted_lengths = jnp.where(is_home, own_lengths, core_swap(own_lengths))
    total = n * local_rows
    ends = jnp.cumsum(hosted_lengths)
    positions = jnp.arange(total, dtype=jnp.int32)
    starts = jnp.max(
        jnp.where(positions[:, None] >= ends[None, :], ends[None, :], 0), axis=1, keepdims=True
    ).astype(jnp.int32)
    block = jnp.arange(total // rows, dtype=jnp.int32)
    low = starts[::rows, 0] // rows
    shard = (block // 2) ^ z
    held = ((block & 1) ^ c) * n + shard
    sent = 2 * (shard ^ (c * half)) + (block & 1)
    tables = (low, held, sent)
    slopes = cross(bias_slope)

    items, crossed, piece, tables, starts, slopes = barrier(
        (items, crossed, piece, tables, starts, slopes)
    )

    def dp_double(x, bit, axis):
        other = dp_swap(x, bit)
        up = (dp & bit) != 0
        return jnp.concatenate(
            [jnp.where(up, other, x), jnp.where(up, x, other)], axis=axis
        )

    side = width // 2
    pair = [piece[:, :side], piece[:, side:]]
    pair = [x.reshape([1] * len(bits) + [slab_w, side]) for x in pair]

    def weights_step(pair, k):
        there, here = bits[:0:-1], bits[1:]
        return [
            dp_double(pair[0], there[k], bits.index(there[k])),
            dp_double(pair[1], here[k], bits.index(here[k])),
        ]

    def spread(x):
        found = {half: x}
        bit = 1
        while bit < half:
            for t in sorted(found):
                found[t ^ bit] = z_swap(found[t], bit)
            bit *= 2
        return found

    middle = rows // 2
    upper = spread(crossed[:middle])
    for k in range(len(bits) - 2):
        pair = weights_step(pair, k)
    upper, pair, lower = barrier((upper, pair, crossed[middle:rows]))
    lower = spread(lower)
    pair = weights_step(pair, len(bits) - 2)
    items, upper, lower, pair = barrier((items, upper, lower, pair))
    piece = dp_double(jnp.concatenate(pair, axis=-1), bits[0], 0)
    piece = piece.reshape(3 * part, width)
    for t in upper:
        items[t] = jnp.concatenate([upper[t], lower[t]], axis=0)
    mine = [items[t] for t in range(n)]
    theirs = [core_swap(x) for x in mine]

    slabs = jnp.concatenate(
        [
            lax.dynamic_slice_in_dim(gate_rows, dp * slab_o, slab_o, 0),
            lax.dynamic_slice_in_dim(proj_out.reshape(part, width), dp * slab_o, slab_o, 0),
        ],
        axis=0,
    )
    everything = lax.all_gather(slabs, AXES).reshape(n_dp, n, 2, slab_o, width)

    w_qkv = jnp.where(c == 0, w_own, piece)

    *attended, act, pre = attend(
        nh, dim, rows, tables, slopes, starts, w_qkv, mine + theirs
    )
    w_gate, w_out, pre_gate, d_gated = prepare(
        n, n_dp, slab_o, z, everything, normed, cotangent, attended[0]
    )
    mine, theirs, attended = barrier((mine, theirs, attended))
    gathered = jnp.concatenate(mine + theirs, axis=0)
    arrived = [
        move(attended[r], send_target(r)) for r in range(n)
    ]
    arrived, w_gate, w_out, pre_gate, d_gated = barrier(
        (arrived, w_gate, w_out, pre_gate, d_gated)
    )
    d_attended, both, gated, d_pre_gate = gate_and_norm(
        n, pre_gate, d_gated, normed, cotangent, arrived
    )

    def add(x, y):
        return (x.astype(F32) + y.astype(F32)).astype(BF)

    order = bits[1:] + bits[:1]
    split = [2] * len(bits)
    forth, back = bits[1:], bits[:0:-1]

    def reduce_bit(x, b, axis):
        up = (dp & b) != 0
        low_half = lax.slice_in_dim(x, 0, 1, axis=axis)
        high_half = lax.slice_in_dim(x, 1, 2, axis=axis)
        return add(
            jnp.where(up, high_half, low_half),
            dp_swap(jnp.where(up, low_half, high_half), b),
        )

    def double_bit(x, b, axis):
        other = dp_swap(x, b)
        up = (dp & b) != 0
        return jnp.concatenate(
            [jnp.where(up, other, x), jnp.where(up, x, other)], axis=axis
        )

    both = both.reshape([2, n] + split + [slab_o, width])
    both = reduce_bit(both, 1, 1 + len(bits))
    arrived = [
        move(d_attended[r], back_target(r)) for r in range(n)
    ]
    d_att = jnp.concatenate(arrived, axis=0)
    pair = [both[0], both[1]]
    def reduce_pair(pair, k, first_axis):
        return [
            reduce_bit(pair[0], forth[k], first_axis + order.index(forth[k])),
            reduce_bit(pair[1], back[k], first_axis + order.index(back[k])),
        ]

    both = reduce_pair(pair, 0, 1)
    mixed = (token_single + dot(gated, w_out)).astype(BF)
    d_normed_gate = dot(d_pre_gate, w_gate)
    d_att, both, mixed, d_normed_gate = barrier((d_att, both, mixed, d_normed_gate))
    for k in range(1, len(forth)):
        both = reduce_pair(both, k, 1)

    d_pre, slope_rows = attend_back(
        nh, dim, rows, tables, slopes, starts, act, pre, d_att
    )

    def partial(first_block, last_block):
        return dot(d_pre[first_block * rows : last_block * rows], w_qkv).astype(BF)

    d_pre, both = barrier((d_pre, both))
    theirs = partial(n, 2 * n)
    got = core_swap(theirs)
    d_pre, theirs = barrier((d_pre, theirs))
    in_part = dot(d_pre, gathered, TN).astype(BF)
    mine = partial(0, n)
    both = jnp.stack(both).reshape(2, n, slab_o, width)
    both = add(both[:, :half], z_swap(both[:, half:], half))
    in_part, got, both = barrier((in_part, got, both))

    side = width // 2
    x = in_part.reshape(split + [slab_w, width])
    pair = reduce_pair([x[..., :side], x[..., side:]], 0, 0)
    home, away = add(mine[: half * rows], got[: half * rows]), add(
        mine[half * rows :], got[half * rows :]
    )
    bit = half // 2
    while bit >= 1:
        away = add(away[: bit * rows], z_swap(away[bit * rows :], bit))
        bit //= 2
    bit = half // 2
    while bit >= 1:
        both = add(both[:, :bit], z_swap(both[:, bit:], bit))
        bit //= 2
    both = both.reshape(2 * slab_o, width)
    for k in range(1, len(forth)):
        pair = reduce_pair(pair, k, 0)
    pair, away, home, both = barrier((pair, away, home, both))

    cuts = [away[k * rows // 4 : (k + 1) * rows // 4] for k in range(4)]
    moved = [z_swap(cuts[0], half)]
    x = cross(jnp.concatenate(pair, axis=-1))
    x, moved, home, both, cuts = barrier((x, moved, home, both, cuts))

    moved.append(z_swap(cuts[1], half))
    x = reduce_bit(x, 1, len(bits) - 1)
    bit = half // 2
    while bit > 1:
        home = add(home[: bit * rows], z_swap(home[bit * rows :], bit))
        bit //= 2
    homes = [home[:middle]]
    if bit:
        homes[0] = add(homes[0], z_swap(home[rows : rows + middle], 1))
    x, moved, cuts, homes, home = barrier((x, moved, cuts, homes, home))
    homes.append(home[middle:rows])
    if bit:
        homes[1] = add(homes[1], z_swap(home[rows + middle :], 1))
    moved.append(z_swap(cuts[2], half))
    x = x.reshape(slab_w, width)
    place = sum(
        jnp.where((dp & b) != 0, 1 << (len(bits) - 1 - i), 0) for i, b in enumerate(order)
    )
    own = jnp.concatenate(
        [
            lax.dynamic_slice_in_dim(w_own, place * slab_w, slab_w, 0),
            lax.dynamic_slice_in_dim(gate_rows, place * slab_o, slab_o, 0),
        ],
        axis=0,
    )
    x = jnp.concatenate([x, both], axis=0)
    gain_part = jnp.sum(x[: slab_w + slab_o].astype(F32) * own.astype(F32), axis=0)
    own_slope = jnp.sum(slope_rows, axis=(1, 2))
    chunk = z ^ (c * half)
    slope_part = jnp.where(jnp.arange(n)[:, None] == chunk, own_slope[None, :], 0.0)
    slope_part = jnp.pad(slope_part.reshape(-1), (0, width - n * nh))
    small = jnp.stack([gain_part, slope_part])
    high = small.astype(BF)
    rest = (small - high.astype(F32)).astype(BF)
    x = jnp.concatenate([x, high, rest, jnp.zeros((12, width), BF)], axis=0)
    x = x.reshape([1] * len(bits) + list(x.shape))

    def double_pair(pair, k):
        return [
            double_bit(pair[0], back[k], order.index(back[k])),
            double_bit(pair[1], forth[k], order.index(forth[k])),
        ]

    pair = double_pair([x[..., :side], x[..., side:]], 0)
    pair, moved, cuts, homes = barrier((pair, moved, cuts, homes))
    home = jnp.concatenate(homes, axis=0)
    moved.append(z_swap(cuts[3], half))
    for k in range(1, len(forth)):
        pair = double_pair(pair, k)
    pair, moved = barrier((pair, moved))
    away = jnp.concatenate(moved, axis=0)
    keep = jnp.where(is_home, home, away)
    got = core_swap(jnp.where(is_home, away, home))
    d_normed = jnp.concatenate(
        [jnp.where(c == 0, keep, got), jnp.where(c == 0, got, keep)], axis=0
    ).astype(F32) + d_normed_gate
    pair = [
        double_bit(y, 1, len(bits) - 1).reshape(n_dp, 5 * slab_o + 16, side) for y in pair
    ]
    grad_proj_in, grad_proj_out = assemble(nh, dim, n_dp, width, *pair)
    grad_proj_in = grad_proj_in.reshape(width, nh, 4, dim)
    grad_proj_out = grad_proj_out.reshape(nh, dim, width)

    small = jnp.concatenate([y[:, 5 * slab_o :] for y in pair], axis=-1).astype(F32)
    small = jnp.sum(small, axis=0)
    small = small[:2] + small[2:4]
    small = small + sum(z_swap(small, t) for t in range(1, n))
    norm_gain_gradient = small[0] / input_norm_gain
    grad_slope = lax.dynamic_slice_in_dim(small[1], z * nh, nh, 0)

    dh = d_normed * input_norm_gain
    token_gradient = cotangent.astype(F32) + inverse_deviation * (
        dh
        - jnp.mean(dh, axis=1, keepdims=True)
        - xhat * jnp.mean(dh * xhat, axis=1, keepdims=True)
    )
    return (mixed, token_gradient, norm_gain_gradient, grad_proj_in, grad_proj_out, grad_slope)


def solution(mesh):
    return jax.shard_map(
        functools.partial(body, mesh.shape["dp"], mesh.shape["head"]),
        mesh=mesh,
        in_specs=(
            P(("dp", "head"), None),
            P(),
            P(None, "head", None, None),
            P("head", None, None),
            P("head"),
            P("dp", None),
            P(("dp", "head"), None),
        ),
        out_specs=(
            P(("dp", "head"), None),
            P(("dp", "head"), None),
            P(),
            P(None, "head", None, None),
            P("head", None, None),
            P("head"),
        ),
        check_vma=False,
    )
```
